512 devices in a mesh: wide: 32 (over y, z_hi, core), ctx: 16 (over x, z_lo).
Axes of the slice: x: 4, y: 8, z: 8 (z_hi: 2, z_lo: 4; z = z_hi * 4 + z_lo), core: 2. Of those that a mesh axis runs over, the one named last changes fastest.
Arguments:
- q_pol: bfloat16 [32, 2048, 2048], P('wide', 'ctx'), may hold values from -24 to 24
- k_pol: bfloat16 [32, 2048, 512], P('wide', 'ctx'), may hold values from -24 to 24
- v_pol: bfloat16 [32, 2048, 512], P('wide', 'ctx'), may hold values from -6 to 6
- d_out: bfloat16 [32, 2048, 2048], P('wide', 'ctx'), may hold values from -6 to 6
- h_ref: bfloat16 [32, 2048, 4096], P('wide', 'ctx'), may hold values from -400 to 400
- norm_gain: bfloat16 [4096], replicated, may hold values from 0.5 to 1.5
- w_kv_ref: bfloat16 [4096, 1024], P('wide'), may hold values from -0.09375 to 0.09375
- lengths: int32 [32, 4], P('wide'), may hold values from 1 to 1024, 2048 in all within a row
- block_map: int32 [16, 2], replicated, may hold values from 0 to 31, as said below
Outputs:
- d_query: float32 [32, 2048, 2048], P('wide', 'ctx')
- d_key: float32 [32, 2048, 512], P('wide', 'ctx')
- d_value: float32 [32, 2048, 512], P('wide', 'ctx')
- k_ref: bfloat16 [32, 2048, 512], P('wide', 'ctx')
- v_ref: bfloat16 [32, 2048, 512], P('wide', 'ctx')
The draws below stay inside these ranges and needn't reach their ends.
Inputs may be any that keep to these rules, and one draw needn't show every extreme that they name: Each row of block_map is j and 31 - j; its first column holds each of 0 to 15 once.
All inputs are finite; a program needn't handle non-finite values.
Results may differ from the reference program's by a relative error of at most 0.018.
Values may be sent and summed in bfloat16 or wider, within the bound.
A program may use at most 128 MiB of HBM per device.

```python
import math
import jax
import jax.numpy as jnp
import numpy as np
from jax import lax

D = 4096
HEADS = 16
KV_HEADS = 4
HEAD_DIM = 128
ROLL = 4
TOK_DEV = 128
LENGTH = 2048
SEQS = 32
QW = 2048
KVW = 512
N_CTX = 16


def shared_keys(key):
    return jnp.clip(jax.random.normal(key, (SEQS, LENGTH, KV_HEADS * HEAD_DIM), jnp.float32), -4.5, 4.5)


def draw_q_pol(key, part):
    key = jax.random.fold_in(key, 11)
    shape = (SEQS, LENGTH, HEADS * HEAD_DIM)
    values = jnp.clip(jax.random.normal(key, shape, jnp.float32), -6.0, 6.0)
    return values.astype(jnp.bfloat16)


def draw_k_pol(key, part):
    common = shared_keys(key)
    values = common
    return values.astype(jnp.bfloat16)


def draw_h_ref(key, part):
    key = jax.random.fold_in(key, 23)
    key_base, key_rows, key_cols = jax.random.split(key, 3)
    shape = (SEQS, LENGTH, D)
    base = jnp.clip(jax.random.normal(key_base, shape, jnp.float32), -3.9, 3.9)
    top = math.log(10.0)
    bottom = 0.0
    row_scale = jnp.exp(jax.random.uniform(key_rows, (SEQS, LENGTH, 1), jnp.float32, bottom, top))
    col_scale = jnp.exp(jax.random.uniform(key_cols, (1, 1, D), jnp.float32, bottom, top))
    return (base * row_scale * col_scale).astype(jnp.bfloat16)


def draw_block_map(key, part):
    key = jax.random.fold_in(key, 17)
    order = jax.random.permutation(key, N_CTX).astype(jnp.int32)
    return jnp.stack([order, 2 * N_CTX - 1 - order], axis=1).astype(jnp.int32)


def steps_of(rng, dims, pieces, smallest, top_value):
    level, own = 1.0, jax.random.fold_in(rng, 6)
    for axis_at, blocks in pieces:
        heights = jnp.exp(jax.random.uniform(jax.random.fold_in(own, axis_at), (blocks,), jnp.float32, smallest / len(pieces), top_value / len(pieces)))
        level = level * jnp.repeat(heights, dims[axis_at] // blocks).reshape([-1 if axis == axis_at else 1 for axis in range(len(dims))])
    return level


def split_up(count, total, bound, slope):
    weights = [(1 << 20) // math.isqrt(standing ** slope) + 1 for standing in range(2, count + 1)]
    spare, counts = total - bound - (count - 1), [1] * (count - 1)
    while spare > 0:
        candidates = [i for i in range(count - 1) if counts[i] < bound]
        whole, remaining = sum([weights[i] for i in candidates]), spare
        for i in candidates:
            extra = min(bound - counts[i], max(1, remaining * weights[i] // whole), spare)
            counts[i] = counts[i] + extra
            spare = spare - extra
    return np.array([bound] + counts)


def ragged(rng, count, total, reach, lean):
    if count == 2:
        one = jax.random.randint(rng, (), max(1, total - reach), min(reach, total - 1) + 1)
        return jnp.stack([one, total - one])
    sizes = jnp.asarray(split_up(count, total, reach, lean), jnp.int32)
    twos = (count - 1) // 2
    source_of, taker = sizes[1:1 + 2 * twos:2], sizes[2:2 + 2 * twos:2]
    margin = jnp.minimum(source_of - 1, reach - taker)
    shifted = jax.random.randint(jax.random.fold_in(rng, 1), (twos,), 0, 1 << 20) % (margin + 1)
    sizes = sizes.at[1:1 + 2 * twos:2].set(source_of - shifted).at[2:2 + 2 * twos:2].set(taker + shifted)
    return sizes[jax.random.permutation(jax.random.fold_in(rng, 2), count)]


def scatter_about(own_key, dims, scale, bound, pieces=(), kind=jnp.bfloat16):
    result = jax.random.normal(own_key, dims, jnp.float32) * scale
    if len(pieces) > 0:
        result = steps_of(own_key, dims, pieces, -0.22, 0.18) * result
    return jnp.clip(result, min=-bound, max=bound).astype(kind)


def setup_inputs(seed: int = 0) -> dict:
    key_list = jax.random.split(jax.random.key(seed), 10)
    q_pol = draw_q_pol(jax.random.fold_in(key_list[9], 71), 0)
    k_pol = draw_k_pol(jax.random.fold_in(key_list[9], 71), 0)
    v_pol = scatter_about(key_list[2], (SEQS, LENGTH, KVW), 1.0, 6.0, ((0, 32), (1, 16)))
    d_out = scatter_about(key_list[3], (SEQS, LENGTH, QW), 1.0, 6.0, ((0, 32), (1, 16)))
    h_ref = draw_h_ref(jax.random.fold_in(key_list[9], 71), 0)
    norm_gain = jnp.clip(1.0 + 0.1 * jax.random.normal(key_list[5], (D,), jnp.float32), 0.5, 1.5).astype(jnp.bfloat16)
    w_kv_ref = scatter_about(key_list[6], (D, 2 * KVW), D ** -0.5, 0.09375, ((0, 32),))
    lengths = jax.vmap(lambda own: ragged(own, ROLL, LENGTH, LENGTH // 2, 1))(jax.random.split(key_list[7], SEQS)).reshape((SEQS, ROLL)).astype(jnp.int32)
    block_map = draw_block_map(jax.random.fold_in(key_list[9], 71), 0)
    return {"q_pol": q_pol, "k_pol": k_pol, "v_pol": v_pol, "d_out": d_out, "h_ref": h_ref, "norm_gain": norm_gain, "w_kv_ref": w_kv_ref, "lengths": lengths, "block_map": block_map}


def positions(block_map):
    all_rows = jnp.arange(LENGTH, dtype=jnp.int32)
    half_rows = TOK_DEV // 2
    device_index = (all_rows // TOK_DEV).astype(jnp.int32)
    side_index = (all_rows % TOK_DEV // half_rows).astype(jnp.int32)
    return (block_map[device_index, side_index] * half_rows + all_rows % half_rows).astype(jnp.int32)

def documents(lengths_row, places):
    doc_ends = jnp.cumsum(lengths_row).astype(jnp.int32)
    return lax.optimization_barrier(jnp.sum((places[:, None] >= doc_ends[None, :]).astype(jnp.int32), axis=1))

def lowered(values):
    return lax.optimization_barrier(values.astype(jnp.bfloat16)).astype(jnp.float32)

def reference(q_pol, k_pol, v_pol, d_out, h_ref, norm_gain, w_kv_ref, lengths, block_map):
    places = positions(block_map)
    group_size = HEADS // KV_HEADS
    score_scale = HEAD_DIM ** (-0.5)
    key_width = KV_HEADS * HEAD_DIM

    def one_sequence(items):
        queries, keys, values, grads, lengths_row = items
        segment = documents(lengths_row, places)
        visible = (places[None, :] <= places[:, None]) & (segment[None, :] == segment[:, None])
        dq_parts = []
        dk_parts = []
        dv_parts = []
        for head_group in range(KV_HEADS):
            wide_lo = head_group * group_size * HEAD_DIM
            wide_hi = wide_lo + group_size * HEAD_DIM
            narrow_lo = head_group * HEAD_DIM
            narrow_hi = narrow_lo + HEAD_DIM
            q_block = queries[:, wide_lo:wide_hi].astype(jnp.float32).reshape(LENGTH, group_size, HEAD_DIM)
            o_grad = grads[:, wide_lo:wide_hi].astype(jnp.float32).reshape(LENGTH, group_size, HEAD_DIM)
            k_block = keys[:, narrow_lo:narrow_hi].astype(jnp.float32)
            v_block = values[:, narrow_lo:narrow_hi].astype(jnp.float32)
            scores = jnp.einsum('thd,cd->htc', q_block, k_block) * score_scale
            scores = jnp.where(visible[None], scores, jnp.float32(-1e+30))
            row_top = lax.optimization_barrier(jnp.max(scores, axis=-1, keepdims=True))
            expons = jnp.exp(scores - row_top)
            probs = expons / lax.optimization_barrier(jnp.sum(expons, axis=-1, keepdims=True))
            probs_low = lowered(probs)
            d_probs = jnp.einsum('thd,cd->htc', o_grad, v_block)
            row_delta = lax.optimization_barrier(jnp.sum(probs_low * d_probs, axis=-1, keepdims=True))
            d_scores = lowered(probs * (d_probs - row_delta))
            dq_block = jnp.einsum('htc,cd->thd', d_scores, k_block) * score_scale
            dq_parts.append(dq_block.reshape(LENGTH, group_size * HEAD_DIM))
            score_split = d_scores.reshape(group_size, N_CTX, TOK_DEV, LENGTH)
            prob_split = probs_low.reshape(group_size, N_CTX, TOK_DEV, LENGTH)
            query_split = q_block.reshape(N_CTX, TOK_DEV, group_size, HEAD_DIM)
            grad_split = o_grad.reshape(N_CTX, TOK_DEV, group_size, HEAD_DIM)
            key_terms = jnp.einsum('gdtc,dtgh->dch', score_split, query_split) * score_scale
            value_terms = jnp.einsum('gdtc,dtgh->dch', prob_split, grad_split)
            dk_parts.append(lax.optimization_barrier(jnp.sum(lowered(key_terms), axis=0)))
            dv_parts.append(lax.optimization_barrier(jnp.sum(lowered(value_terms), axis=0)))
        return (jnp.concatenate(dq_parts, axis=-1), jnp.concatenate(dk_parts, axis=-1), jnp.concatenate(dv_parts, axis=-1))
    d_query, d_key, d_value = lax.map(one_sequence, (q_pol, k_pol, v_pol, d_out, lengths))
    activations = h_ref.astype(jnp.float32)
    mean_square = lax.optimization_barrier(jnp.mean(activations * activations, axis=-1, keepdims=True))
    normed = (activations * lax.rsqrt(mean_square + 1e-05) * norm_gain.astype(jnp.float32)).astype(jnp.bfloat16)
    projected = jnp.dot(normed.reshape(SEQS * LENGTH, D), w_kv_ref, preferred_element_type=jnp.float32)
    projected = projected.astype(jnp.bfloat16).reshape(SEQS, LENGTH, 2 * key_width)
    return (d_query, d_key, d_value, projected[:, :, :key_width], projected[:, :, key_width:])
```

```python
import functools
import jax
import jax.numpy as jnp
from jax import lax
from jax.experimental import pallas as pl
from jax.experimental.pallas import tpu as pltpu
from jax.sharding import PartitionSpec as P

MESH = pl.DeviceIdType.MESH
HD = 128
NX, NZ, NY = 4, 4, 8
GROUP = 4
ROWS = 128
HALF = 64
SCALE = HD ** -0.5
TK = 256
PAD = TK - HALF
NEG = -1e30
MIB = 1 << 20


def wrap(value, size):
    return lax.rem(value + size, size)


def place():
    wide = lax.axis_index("wide")
    ctx = lax.axis_index("ctx")
    return wide // 4, (wide // 2) % 2, wide % 2, ctx // NZ, ctx % NZ


def wide_id(y, zh, core):
    return (y * 2 + zh) * 2 + core


def ctx_peers(x, zl):
    peers = []
    for dz in (2, 1, 3, 0):
        for dx in (2, 1, 3, 0):
            if dz or dx:
                peers.append((wrap(x + dx, NX), wrap(zl + dz, NZ)))
    return peers


def meet(ids):
    barrier = pltpu.get_barrier_semaphore()
    for ident in ids:
        pl.semaphore_signal(barrier, inc=1, device_id=ident, device_id_type=MESH)
    pl.semaphore_wait(barrier, len(ids))


def remote(src, dst, sems, slot, ident):
    send, recv = sems
    return pltpu.make_async_remote_copy(
        src_ref=src, dst_ref=dst, send_sem=send.at[slot], recv_sem=recv.at[slot],
        device_id=ident, device_id_type=MESH,
    )


class WeightRing:
    def __init__(self, own, held, ring_sems, core_sems, core_dst=None):
        y, zh, core, x, zl = place()
        ctx = lax.axis_index("ctx")
        self.y, self.core = y, core
        self.own, self.held = own, held
        self.ring_sems, self.core_sems = ring_sems, core_sems
        self.right = (wide_id(wrap(y + 1, NY), zh, core), ctx)
        self.left = (wide_id(wrap(y - 1, NY), zh, core), ctx)
        self.other = (wide_id(y, zh, 1 - core), ctx)
        self.sent = []
        self.core_copies = []

    def chunk(self, owner, core, part):
        start = pl.multiple_of(core * ROWS + part * HALF, HALF)
        return self.held.at[owner, pl.ds(start, HALF)]

    def ring_copy(self, way, step, part):
        owner = wrap(self.y - (step - 1), NY) if way == 0 else wrap(self.y + (step - 1), NY)
        if step == 1:
            src = self.own.at[pl.ds(part * HALF, HALF)]
        else:
            src = self.chunk(owner, self.core, part)
        slot = (step - 1) * 4 + way * 2 + part
        return remote(src, self.chunk(owner, self.core, part), self.ring_sems, slot,
                      self.right if way == 0 else self.left)

    def arrival(self, way, step, part):
        owner = wrap(self.y - step, NY) if way == 0 else wrap(self.y + step, NY)
        dst = self.chunk(owner, self.core, part)
        slot = (step - 1) * 4 + way * 2 + part
        return remote(dst, dst, self.ring_sems, slot, self.right if way == 0 else self.left)

    def core_slot(self, way, step, part):
        return (step - 1) * 4 + way * 2 + part + 2

    def to_core(self, src, owner, part, slot):
        copy = remote(src, self.chunk(owner, self.core, part), self.core_sems, slot, self.other)
        copy.start()
        self.core_copies.append((copy, owner, part, slot))

    def valid(self, way, step, part):
        return step < 4 or (step == 4 and part == way)

    def begin(self):
        for part in range(2):
            for way in range(2):
                copy = self.ring_copy(way, 1, part)
                copy.start()
                self.sent.append(copy)
        for part in range(2):
            self.to_core(self.own.at[pl.ds(part * HALF, HALF)], self.y, part, part)

    def advance(self, step):
        for part in range(2):
            for way in range(2):
                if self.valid(way, step, part):
                    self.arrival(way, step, part).wait_recv()
                    if self.valid(way, step + 1, part):
                        copy = self.ring_copy(way, step + 1, part)
                        copy.start()
                        self.sent.append(copy)
                    owner = wrap(self.y - step, NY) if way == 0 else wrap(self.y + step, NY)
                    self.to_core(self.chunk(owner, self.core, part), owner, part, self.core_slot(way, step, part))

    def wait_core(self, copies):
        for copy, owner, part, slot in copies:
            dst = self.chunk(owner, 1 - self.core, part)
            remote(dst, dst, self.core_sems, slot, self.other).wait_recv()

    def finish_sends(self):
        for copy in self.sent:
            copy.wait_send()
        for copy, _, _, _ in self.core_copies:
            copy.wait_send()


def gather_kernel(q, k, v, do, w, q_in, do_in, kv_in, held, other_w,
                  x_send, x_recv, kv_send, kv_recv, ring_send, ring_recv, core_send, core_recv, zh_send, zh_recv,
                  local_sem):
    y, zh, core, x, zl = place()
    wide = lax.axis_index("wide")
    ctx = lax.axis_index("ctx")
    ring = WeightRing(w, held, (ring_send, ring_recv), (core_send, core_recv))
    across = (wide_id(y, 1 - zh, core), x * NZ + (NZ - 1 - zl))
    inner = (wide, x * NZ + 1 + zl // 3)
    edge = (zl == 0) | (zl == NZ - 1)
    peers = ctx_peers(x, zl)
    meet([(wide, px * NZ + pz) for px, pz in peers] + [ring.right, ring.left, ring.other, across])

    to_across = remote(w, other_w, (zh_send, zh_recv), 0, across)
    to_inner = remote(other_w, other_w, (zh_send, zh_recv), 1, inner)
    pl.when(edge)(to_across.start)
    ring.begin()

    def cols(index, width):
        return pl.ds(pl.multiple_of(index * width, width), width)

    copies = []
    for n, (px, pz) in enumerate(peers):
        for j, src in enumerate((k, v)):
            copy = remote(src.at[0, :, cols(px, HD)], kv_in.at[ctx, j], (kv_send, kv_recv), 2 * n + j, (wide, px * NZ + pz))
            copy.start()
            copies.append(copy)
    for n, dx in enumerate((2, 1, 3)):
        px = wrap(x + dx, NX)
        for j, (src, dst) in enumerate(((q, q_in), (do, do_in))):
            copy = remote(src.at[0, :, cols(px, GROUP * HD)], dst.at[x], (x_send, x_recv), 2 * n + j, (wide, px * NZ + zl))
            copy.start()
            copies.append(copy)
    local = [
        pltpu.make_async_copy(q.at[0, :, cols(x, GROUP * HD)], q_in.at[x], local_sem.at[0]),
        pltpu.make_async_copy(do.at[0, :, cols(x, GROUP * HD)], do_in.at[x], local_sem.at[1]),
        pltpu.make_async_copy(k.at[0, :, cols(x, HD)], kv_in.at[ctx, 0], local_sem.at[2]),
        pltpu.make_async_copy(v.at[0, :, cols(x, HD)], kv_in.at[ctx, 1], local_sem.at[3]),
        pltpu.make_async_copy(w, held.at[y, pl.ds(pl.multiple_of(core * ROWS, ROWS), ROWS)], local_sem.at[4]),
    ]
    for copy in local:
        copy.start()

    @pl.when(edge)
    def _():
        to_across.wait_recv()
        to_inner.start()

    for step in range(1, 5):
        ring.advance(step)

    @pl.when(edge)
    def _():
        to_across.wait_send()
        to_inner.wait_send()

    @pl.when(jnp.logical_not(edge))
    def _():
        to_inner.wait_recv()

    for copy in copies:
        copy.wait()
    ring.wait_core(ring.core_copies)
    ring.finish_sends()
    for copy in local:
        copy.wait()


def attend_kernel(map_ref, len_ref, q_in, do_in, kv_in, dq_out, terms, kpos, vpos, dkpos, dvpos, s_ref, g_ref):
    zl = lax.axis_index("ctx") % NZ
    kpos[pl.ds(0, PAD)] = jnp.zeros((PAD, HD), jnp.bfloat16)
    vpos[pl.ds(0, PAD)] = jnp.zeros((PAD, HD), jnp.bfloat16)
    dkpos[...] = jnp.zeros_like(dkpos)
    dvpos[...] = jnp.zeros_like(dvpos)

    def place_block(i, carry):
        for j in range(2):
            at = pl.ds(pl.multiple_of(map_ref[i, j] * HALF + PAD, HALF), HALF)
            kpos[at] = kv_in[i, 0, pl.ds(j * HALF, HALF)]
            vpos[at] = kv_in[i, 1, pl.ds(j * HALF, HALF)]
        return carry

    lax.fori_loop(0, NX * NZ, place_block, 0)
    end0 = len_ref[0, 0]
    end1 = end0 + len_ref[0, 1]
    end2 = end1 + len_ref[0, 2]
    end3 = end2 + len_ref[0, 3]

    def doc_start(pos):
        start = jnp.zeros_like(pos)
        for end in (end0, end1, end2, end3):
            start = jnp.where(pos >= end, end, start)
        return start

    def nt(a, b):
        return lax.dot_general(a, b, (((1,), (1,)), ((), ())), preferred_element_type=jnp.float32)

    def tn(a, b):
        return lax.dot_general(a, b, (((0,), (0,)), ((), ())), preferred_element_type=jnp.float32)

    def row_block(n, carry):
        xs, j = n // 2, n % 2
        block = map_ref[xs * NZ + zl, j]
        base = block * HALF
        start = doc_start(base)
        span = base + HALF - (start // HALF) * HALF
        tiles = (span + TK - 1) // TK
        rows = pl.ds(pl.multiple_of(j * HALF, HALF), HALF)
        q = jnp.concatenate([q_in[xs, rows, h * HD:(h + 1) * HD] for h in range(GROUP)], axis=0)
        do = jnp.concatenate([do_in[xs, rows, h * HD:(h + 1) * HD] for h in range(GROUP)], axis=0)
        pos = base + lax.broadcasted_iota(jnp.int32, (HALF, 1), 0)
        first = doc_start(pos)

        def scores(t, top):
            at = pl.ds(pl.multiple_of(base - t * TK, HALF), TK)
            kp = base - t * TK - PAD + lax.broadcasted_iota(jnp.int32, (HALF, TK), 1)
            bias = jnp.where((kp <= pos) & (kp >= first), 0.0, NEG)
            s = nt(q, kpos[at]) * SCALE
            s = (s.reshape(GROUP, HALF, TK) + bias[None]).reshape(GROUP * HALF, TK)
            s_ref[t] = s
            g_ref[t] = nt(do, vpos[at])
            for c in range(TK // 128):
                top = jnp.maximum(top, s[:, c * 128:(c + 1) * 128])
            return top

        top = lax.fori_loop(0, tiles, scores, jnp.full((GROUP * HALF, 128), NEG, jnp.float32))
        top = jnp.max(top, axis=1, keepdims=True)

        def weigh(t, sums):
            total, delta = sums
            p = jnp.exp(s_ref[t] - top)
            s_ref[t] = p
            pg = p * g_ref[t]
            for c in range(TK // 128):
                total = total + p[:, c * 128:(c + 1) * 128]
                delta = delta + pg[:, c * 128:(c + 1) * 128]
            return total, delta

        zero = jnp.zeros((GROUP * HALF, 128), jnp.float32)
        total, delta = lax.fori_loop(0, tiles, weigh, (zero, zero))
        inverse = 1.0 / jnp.sum(total, axis=1, keepdims=True)
        delta = jnp.sum(delta, axis=1, keepdims=True) * inverse

        def grads(t, dq):
            at = pl.ds(pl.multiple_of(base - t * TK, HALF), TK)
            p = s_ref[t] * inverse
            ds = (p * (g_ref[t] - delta)).astype(jnp.bfloat16)
            dkpos[at] += tn(ds, q)
            dvpos[at] += tn(p.astype(jnp.bfloat16), do)
            return dq + jnp.dot(ds, kpos[at], preferred_element_type=jnp.float32)

        dq = lax.fori_loop(0, tiles, grads, jnp.zeros((GROUP * HALF, HD), jnp.float32))
        dq = (dq * SCALE).astype(jnp.bfloat16)
        for h in range(GROUP):
            dq_out[xs, rows, h * HD:(h + 1) * HD] = dq[h * HALF:(h + 1) * HALF]
        return carry

    lax.fori_loop(0, 2 * NX, row_block, 0)

    def store_block(i, carry):
        for j in range(2):
            at = pl.ds(pl.multiple_of(map_ref[i, j] * HALF + PAD, HALF), HALF)
            terms[i, 0, pl.ds(j * HALF, HALF)] = (dkpos[at] * SCALE).astype(jnp.bfloat16)
            terms[i, 1, pl.ds(j * HALF, HALF)] = dvpos[at].astype(jnp.bfloat16)
        return carry

    lax.fori_loop(0, NX * NZ, store_block, 0)


def return_kernel(dq_out, terms, held, other_w, h, gain, dq, dk, dv, kref, vref,
                  dq_got, terms_got, own_v, far_v, h_v, normed, acc,
                  x_send, x_recv, t_send, t_recv, ring_send, ring_recv, core_send, core_recv, local_sem):
    y, zh, core, x, zl = place()
    wide = lax.axis_index("wide")
    ctx = lax.axis_index("ctx")
    ring = WeightRing(other_w, far_v, (ring_send, ring_recv), (core_send, core_recv))
    load_h = pltpu.make_async_copy(h.at[0], h_v, local_sem.at[0])
    load_w = pltpu.make_async_copy(held, own_v, local_sem.at[1])
    load_h.start()
    load_w.start()
    peers = ctx_peers(x, zl)
    meet([(wide, px * NZ + pz) for px, pz in peers] + [ring.right, ring.left, ring.other])

    ring.begin()
    copies = []
    for n, (px, pz) in enumerate(peers):
        copy = remote(terms.at[px * NZ + pz], terms_got.at[ctx], (t_send, t_recv), n, (wide, px * NZ + pz))
        copy.start()
        copies.append(copy)
    for n, dx in enumerate((2, 1, 3)):
        px = wrap(x + dx, NX)
        copy = remote(dq_out.at[px], dq_got.at[x], (x_send, x_recv), n, (wide, px * NZ + zl))
        copy.start()
        copies.append(copy)
    local = [
        pltpu.make_async_copy(dq_out.at[x], dq_got.at[x], local_sem.at[2]),
        pltpu.make_async_copy(terms.at[ctx], terms_got.at[ctx], local_sem.at[3]),
        pltpu.make_async_copy(other_w, far_v.at[y, pl.ds(pl.multiple_of(core * ROWS, ROWS), ROWS)], local_sem.at[4]),
    ]
    for copy in local:
        copy.start()

    load_h.wait()
    strip = 16

    def norm_rows(i, carry):
        rows = pl.ds(pl.multiple_of(i * strip, strip), strip)
        a = h_v[rows].astype(jnp.float32)
        mean = jnp.mean(a * a, axis=1, keepdims=True)
        normed[rows] = (a * lax.rsqrt(mean + 1e-05) * gain[...].astype(jnp.float32)).astype(jnp.bfloat16)
        return carry

    lax.fori_loop(0, ROWS // strip, norm_rows, 0)
    load_w.wait()
    acc[...] = jnp.zeros_like(acc)

    def project(weights, zh_of, owner):
        at = pl.ds(pl.multiple_of((2 * owner + zh_of) * 2 * ROWS, 2 * ROWS), 2 * ROWS)
        acc[...] += jnp.dot(normed[:, at], weights[owner], preferred_element_type=jnp.float32)

    def near(i, carry):
        project(own_v, zh, i)
        return carry

    lax.fori_loop(0, 4, near, 0)
    ring.advance(1)
    lax.fori_loop(4, 8, near, 0)
    ring.advance(2)
    ring.advance(3)
    ring.advance(4)
    ring.wait_core(ring.core_copies)
    for copy in local:
        copy.wait()

    def far(i, carry):
        project(far_v, 1 - zh, i)
        return carry

    lax.fori_loop(0, NY, far, 0)
    kref[0] = acc[:, :512].astype(jnp.bfloat16)
    vref[0] = acc[:, 512:].astype(jnp.bfloat16)
    for copy in copies:
        copy.wait()
    ring.finish_sends()
    for xs in range(NX):
        dq[0, :, xs * 512:(xs + 1) * 512] = dq_got[xs].astype(jnp.float32)
        for j, out in enumerate((dk, dv)):
            total = terms_got[xs * NZ, j].astype(jnp.float32)
            for zs in range(1, NZ):
                total = total + terms_got[xs * NZ + zs, j].astype(jnp.float32)
            out[0, :, xs * HD:(xs + 1) * HD] = total


def body(q_pol, k_pol, v_pol, d_out, h_ref, norm_gain, w_kv_ref, lengths, block_map):
    bf16, f32 = jnp.bfloat16, jnp.float32
    any_spec = pl.BlockSpec(memory_space=pl.ANY)
    vmem = pl.BlockSpec(memory_space=pltpu.VMEM)
    smem = pl.BlockSpec(memory_space=pltpu.SMEM)
    dma = pltpu.SemaphoreType.DMA
    shape = jax.ShapeDtypeStruct
    q_in, do_in, kv_in, held, other_w = pl.pallas_call(
        gather_kernel,
        name="gather_inputs",
        out_shape=(
            shape((NX, ROWS, GROUP * HD), bf16),
            shape((NX, ROWS, GROUP * HD), bf16),
            shape((NX * NZ, 2, ROWS, HD), bf16),
            shape((NY, 2 * ROWS, 1024), bf16),
            shape((ROWS, 1024), bf16),
        ),
        in_specs=[any_spec] * 5,
        out_specs=(any_spec,) * 5,
        scratch_shapes=[
            dma((6,)), dma((6,)), dma((30,)), dma((30,)), dma((16,)), dma((16,)), dma((18,)), dma((18,)),
            dma((2,)), dma((2,)), dma((5,)),
        ],
        compiler_params=pltpu.CompilerParams(collective_id=0, has_side_effects=True),
    )(q_pol, k_pol, v_pol, d_out, w_kv_ref)
    dq_out, terms = pl.pallas_call(
        attend_kernel,
        name="attend",
        out_shape=(shape((NX, ROWS, GROUP * HD), bf16), shape((NX * NZ, 2, ROWS, HD), bf16)),
        in_specs=[smem, smem, vmem, vmem, vmem],
        out_specs=(vmem, vmem),
        scratch_shapes=[
            pltpu.VMEM((PAD + 2048, HD), bf16),
            pltpu.VMEM((PAD + 2048, HD), bf16),
            pltpu.VMEM((PAD + 2048, HD), f32),
            pltpu.VMEM((PAD + 2048, HD), f32),
            pltpu.VMEM((5, GROUP * HALF, TK), f32),
            pltpu.VMEM((5, GROUP * HALF, TK), f32),
        ],
        compiler_params=pltpu.CompilerParams(vmem_limit_bytes=32 * MIB),
    )(block_map, lengths, q_in, do_in, kv_in)
    return pl.pallas_call(
        return_kernel,
        name="return_results",
        out_shape=(
            shape((1, ROWS, 2048), f32),
            shape((1, ROWS, 512), f32),
            shape((1, ROWS, 512), f32),
            shape((1, ROWS, 512), bf16),
            shape((1, ROWS, 512), bf16),
        ),
        in_specs=[any_spec] * 5 + [vmem],
        out_specs=(vmem,) * 5,
        scratch_shapes=[
            pltpu.VMEM((NX, ROWS, GROUP * HD), bf16),
            pltpu.VMEM((NX * NZ, 2, ROWS, HD), bf16),
            pltpu.VMEM((NY, 2 * ROWS, 1024), bf16),
            pltpu.VMEM((NY, 2 * ROWS, 1024), bf16),
            pltpu.VMEM((ROWS, 4096), bf16),
            pltpu.VMEM((ROWS, 4096), bf16),
            pltpu.VMEM((ROWS, 1024), f32),
            dma((3,)), dma((3,)), dma((15,)), dma((15,)), dma((16,)), dma((16,)), dma((18,)), dma((18,)), dma((5,)),
        ],
        compiler_params=pltpu.CompilerParams(
            collective_id=1, has_side_effects=True, vmem_limit_bytes=48 * MIB
        ),
    )(dq_out, terms, held, other_w, h_ref, norm_gain.reshape(1, -1))


def solution(mesh):
    rows = P("wide", "ctx", None)
    return jax.shard_map(
        body,
        mesh=mesh,
        in_specs=(rows, rows, rows, rows, rows, P(), P("wide", None), P("wide", None), P()),
        out_specs=(rows,) * 5,
        check_vma=False,
    )
```

```python
import functools
import jax
import jax.numpy as jnp
from jax import lax
from jax.experimental import pallas as pl
from jax.experimental.pallas import tpu as pltpu
from jax.sharding import PartitionSpec as P

MESH = pl.DeviceIdType.MESH
HD = 128
NX, NZ, NY = 4, 4, 8
GROUP = 4
ROWS = 128
HALF = 64
SCALE = HD ** -0.5
TK = 256
WINDOW = 1024 + HALF
BACK = WINDOW // HALF - 1
TILES = tuple((off, min(TK, WINDOW - off)) for off in range(0, WINDOW, TK))
NEG = -1e30
LOG2E = 1.4426950408889634
MIB = 1 << 20
VMEM_ALL = 63 * MIB


def wrap(value, size):
    return lax.rem(value + size, size)


def place():
    wide = lax.axis_index("wide")
    ctx = lax.axis_index("ctx")
    return wide // 4, (wide // 2) % 2, wide % 2, ctx // NZ, ctx % NZ


def wide_id(y, zh, core):
    return (y * 2 + zh) * 2 + core


def ctx_peers(x, zl):
    peers = []
    for dz in (2, 1, 3, 0):
        for dx in (2, 1, 3, 0):
            if dz or dx:
                peers.append((wrap(x + dx, NX), wrap(zl + dz, NZ)))
    return peers


def meet(ids):
    barrier = pltpu.get_barrier_semaphore()
    for ident in ids:
        pl.semaphore_signal(barrier, inc=1, device_id=ident, device_id_type=MESH)
    pl.semaphore_wait(barrier, len(ids))


def remote(src, dst, sems, slot, ident):
    send, recv = sems
    return pltpu.make_async_remote_copy(
        src_ref=src, dst_ref=dst, send_sem=send.at[slot], recv_sem=recv.at[slot],
        device_id=ident, device_id_type=MESH,
    )


class WeightRing:
    def __init__(self, own, held, ring_sems, core_sems, core_dst=None):
        y, zh, core, x, zl = place()
        ctx = lax.axis_index("ctx")
        self.y, self.core = y, core
        self.own, self.held = own, held
        self.ring_sems, self.core_sems = ring_sems, core_sems
        self.right = (wide_id(wrap(y + 1, NY), zh, core), ctx)
        self.left = (wide_id(wrap(y - 1, NY), zh, core), ctx)
        self.other = (wide_id(y, zh, 1 - core), ctx)
        self.sent = []
        self.core_copies = []

    def chunk(self, owner, core, part):
        start = pl.multiple_of(core * ROWS + part * HALF, HALF)
        return self.held.at[owner, pl.ds(start, HALF)]

    def ring_copy(self, way, step, part):
        owner = wrap(self.y - (step - 1), NY) if way == 0 else wrap(self.y + (step - 1), NY)
        if step == 1:
            src = self.own.at[pl.ds(part * HALF, HALF)]
        else:
            src = self.chunk(owner, self.core, part)
        slot = (step - 1) * 4 + way * 2 + part
        return remote(src, self.chunk(owner, self.core, part), self.ring_sems, slot,
                      self.right if way == 0 else self.left)

    def arrival(self, way, step, part):
        owner = wrap(self.y - step, NY) if way == 0 else wrap(self.y + step, NY)
        dst = self.chunk(owner, self.core, part)
        slot = (step - 1) * 4 + way * 2 + part
        return remote(dst, dst, self.ring_sems, slot, self.right if way == 0 else self.left)

    def core_slot(self, way, step, part):
        return (step - 1) * 4 + way * 2 + part + 2

    def to_core(self, src, owner, part, slot):
        copy = remote(src, self.chunk(owner, self.core, part), self.core_sems, slot, self.other)
        copy.start()
        self.core_copies.append((copy, owner, part, slot))

    def valid(self, way, step, part):
        return step < 4 or (step == 4 and part == way)

    def begin(self):
        for way in range(2):
            copy = self.ring_copy(way, 1, 0)
            copy.start()
            self.sent.append(copy)
        for part in range(2):
            self.to_core(self.own.at[pl.ds(part * HALF, HALF)], self.y, part, part)

    def begin_second(self):
        for copy in self.sent[:2]:
            copy.wait_send()
        for way in range(2):
            copy = self.ring_copy(way, 1, 1)
            copy.start()
            self.sent.append(copy)

    def advance(self, step):
        for part in range(2):
            for way in range(2):
                if self.valid(way, step, part):
                    self.arrival(way, step, part).wait_recv()
                    if self.valid(way, step + 1, part):
                        copy = self.ring_copy(way, step + 1, part)
                        copy.start()
                        self.sent.append(copy)
                    owner = wrap(self.y - step, NY) if way == 0 else wrap(self.y + step, NY)
                    self.to_core(self.chunk(owner, self.core, part), owner, part, self.core_slot(way, step, part))

    def wait_core(self, copies):
        for copy, owner, part, slot in copies:
            dst = self.chunk(owner, 1 - self.core, part)
            remote(dst, dst, self.core_sems, slot, self.other).wait_recv()

    def finish_sends(self):
        for copy in self.sent[2:]:
            copy.wait_send()
        for copy, _, _, _ in self.core_copies:
            copy.wait_send()


class Line:
    def __init__(self, zl):
        half = zl // 2
        self.partner = zl + 1 - 2 * (zl % 2)
        self.far_inner = 2 - half
        self.far_edge = 3 - 3 * half
        self.edge = (zl == 0) | (zl == NZ - 1)
        self.inner = (zl == 1) | (zl == 2)


def cols(index, width):
    return pl.ds(pl.multiple_of(index * width, width), width)


def dot_nt(a, b):
    return lax.dot_general(a, b, (((1,), (1,)), ((), ())), preferred_element_type=jnp.float32)


def dot_tn(a, b):
    return lax.dot_general(a, b, (((0,), (0,)), ((), ())), preferred_element_type=jnp.float32)


def fold(values, combine):
    parts = [values[i:i + 8] for i in range(0, values.shape[0], 8)]
    while len(parts) > 1:
        parts = [combine(parts[i], parts[i + 1]) if i + 1 < len(parts) else parts[i] for i in range(0, len(parts), 2)]
    return parts[0]


def step_kernel(map_ref, len_ref, q, k, v, do, w, h, gain, dq_got, terms_got, projected,
                q_v, do_v, kv_v, kpos, vpos, s_ref, g_ref, dkw, dvw, terms_v, dq_v, passed,
                near_v, far_v, h_v, normed, acc,
                x_send, x_recv, kx_send, kx_recv, kz_send, kz_recv, relay_send, zh_send, zh_recv,
                dq_send, dq_recv, t_send, t_recv, pass_send, pass_recv, sum_send, sum_recv,
                near_send, near_recv, near_csend, near_crecv, far_send, far_recv, far_csend, far_crecv, local_sem):
    y, zh, core, x, zl = place()
    wide = lax.axis_index("wide")
    line = Line(zl)
    own_rows = pl.ds(pl.multiple_of(core * ROWS, ROWS), ROWS)
    own_slot = zl * NX + x
    loads = [
        pltpu.make_async_copy(k.at[0, :, cols(x, HD)], kv_v.at[own_slot, 0], local_sem.at[0]),
        pltpu.make_async_copy(v.at[0, :, cols(x, HD)], kv_v.at[own_slot, 1], local_sem.at[1]),
        pltpu.make_async_copy(h.at[0], h_v, local_sem.at[2]),
        pltpu.make_async_copy(q.at[0, :, cols(x, GROUP * HD)], q_v.at[x], local_sem.at[3]),
        pltpu.make_async_copy(do.at[0, :, cols(x, GROUP * HD)], do_v.at[x], local_sem.at[4]),
        pltpu.make_async_copy(w, near_v.at[y, own_rows], local_sem.at[5]),
    ]
    for copy in loads:
        copy.start()
    near = WeightRing(w, near_v, (near_send, near_recv), (near_csend, near_crecv))
    far_own = far_v.at[y, own_rows]
    far = WeightRing(far_own, far_v, (far_send, far_recv), (far_csend, far_crecv))
    across = (wide_id(y, 1 - zh, core), x * NZ + (NZ - 1 - zl))
    partner = (wide, x * NZ + line.partner)
    far_inner = (wide, x * NZ + line.far_inner)
    far_z = (line.far_inner, line.far_edge)
    meet([(wide, px * NZ + pz) for px, pz in ctx_peers(x, zl)] + [near.right, near.left, near.other, across])

    kx = {}
    for d in (1, 3, 2):
        px = wrap(x + d, NX)
        for j, src in enumerate((k, v)):
            kx[d, j] = remote(src.at[0, :, cols(px, HD)], kv_v.at[own_slot, j], (kx_send, kx_recv), 2 * (d - 1) + j,
                              (wide, px * NZ + zl))
            kx[d, j].start()
    to_across = remote(w, far_own, (zh_send, zh_recv), 0, across)
    to_inner = remote(far_own, far_own, (zh_send, zh_recv), 1, partner)
    pl.when(line.edge)(to_across.start)
    near.begin()

    def piece(z, d, send_sem, ident):
        slot = z * NX + wrap(x + d, NX)
        return pltpu.make_async_remote_copy(
            src_ref=kv_v.at[slot], dst_ref=kv_v.at[slot], send_sem=send_sem, recv_sem=kz_recv.at[slot],
            device_id=ident, device_id_type=MESH,
        )

    kz = []

    def along(d):
        for n, ident in enumerate((far_inner, partner)):
            copy = piece(zl, d, kz_send.at[2 * d + n], ident)
            copy.start()
            kz.append(copy)

    def arrived(z, d):
        piece(z, d, kz_send.at[0], partner).wait_recv()

    def relay_copy(n, d):
        return piece(far_z[n], d, relay_send.at[2 * d + n], partner)

    def relay(d):
        @pl.when(line.inner)
        def _():
            for n in range(2):
                arrived(far_z[n], d)
                relay_copy(n, d).start()

    loads[0].wait()
    loads[1].wait()
    along(0)
    for d in (1, 3, 2):
        for j in range(2):
            kx[d, j].wait_recv()
        along(NX - d)
    qd = {}
    for d in (1, 3, 2):
        px = wrap(x + d, NX)
        for j, (src, dst) in enumerate(((q, q_v), (do, do_v))):
            qd[d, j] = remote(src.at[0, :, cols(px, GROUP * HD)], dst.at[x], (x_send, x_recv), 2 * (d - 1) + j,
                              (wide, px * NZ + zl))
            qd[d, j].start()
    relay(0)
    near.begin_second()

    kpos[pl.ds(0, BACK)] = jnp.zeros((BACK, HALF, HD), jnp.bfloat16)
    vpos[pl.ds(0, BACK)] = jnp.zeros((BACK, HALF, HD), jnp.bfloat16)
    relay(3)
    near.advance(1)

    @pl.when(line.edge)
    def _():
        to_across.wait_recv()
        to_inner.start()

    relay(1)
    loads[2].wait()
    strip = 16

    def norm_rows(i, carry):
        rows = pl.ds(pl.multiple_of(i * strip, strip), strip)
        a = h_v[rows].astype(jnp.float32)
        mean = jnp.mean(a * a, axis=1, keepdims=True)
        normed[rows] = (a * lax.rsqrt(mean + 1e-05) * gain[...].astype(jnp.float32)).astype(jnp.bfloat16)
        return carry

    lax.fori_loop(0, ROWS // strip, norm_rows, 0)
    acc[...] = jnp.zeros_like(acc)
    near.advance(2)
    relay(2)

    def project(weights, zh_of, owner):
        at = pl.ds(pl.multiple_of((2 * owner + zh_of) * 2 * ROWS, 2 * ROWS), 2 * ROWS)
        acc[...] += jnp.dot(normed[:, at], weights[owner], preferred_element_type=jnp.float32)

    def project_near(i, carry):
        project(near_v, zh, wrap(y + i - 2 + NY, NY))
        return carry

    def project_far(i, carry):
        project(far_v, 1 - zh, wrap(y + i - 2 + NY, NY))
        return carry

    @pl.when(line.edge)
    def _():
        for d in (0, 3, 1, 2):
            for n in range(2):
                arrived(far_z[n], d)

    for d in range(NX):
        arrived(line.partner, d)

    def place_block(p, carry):
        slot = jnp.int32(0)
        for i in range(NX * NZ):
            slot = jnp.where(map_ref[0, i] == p, (i % NZ) * NX + i // NZ, slot)
        for j, dst in enumerate((kpos, vpos)):
            pair = kv_v[slot, j]
            dst[BACK + p] = pair[:HALF]
            dst[BACK + 2 * NX * NZ - 1 - p] = pair[HALF:]
        return carry

    lax.fori_loop(0, NX * NZ, place_block, 0)
    ends = [len_ref[0, 0]]
    for i in range(1, 4):
        ends.append(ends[-1] + len_ref[0, i])

    def doc_start(pos):
        start = jnp.zeros_like(pos)
        for end in ends:
            start = jnp.where(pos >= end, end, start)
        return start

    def row_block(d, j):
        xs = wrap(x + d, NX)
        n = 2 * d + j
        block = map_ref[j, xs * NZ + zl]
        base = block * HALF
        rows = pl.ds(pl.multiple_of(j * HALF, HALF), HALF)
        qb = jnp.concatenate([q_v[xs, rows, i * HD:(i + 1) * HD] for i in range(GROUP)], axis=0)
        dob = jnp.concatenate([do_v[xs, rows, i * HD:(i + 1) * HD] for i in range(GROUP)], axis=0)
        lane = lax.broadcasted_iota(jnp.int32, (1, GROUP * HALF), 1)
        pos = base + lane % HALF
        first = doc_start(pos)
        top = jnp.full((8, GROUP * HALF), NEG, jnp.float32)

        def tile(ref, off, size):
            first_block = block + (WINDOW - off - size) // HALF
            parts = [ref[first_block + i] for i in range(size // HALF)]
            return jnp.concatenate(parts, axis=0) if len(parts) > 1 else parts[0]

        for off, size in TILES:
            kp = base + HALF - off - size + lax.broadcasted_iota(jnp.int32, (size, GROUP * HALF), 0)
            s = jnp.where((kp <= pos) & (kp >= first), dot_nt(tile(kpos, off, size), qb), NEG)
            s_ref[off:off + size] = s
            g_ref[off:off + size] = dot_nt(tile(vpos, off, size), dob)
            top = jnp.maximum(top, fold(s, jnp.maximum))
        top = jnp.max(top, axis=0, keepdims=True)
        total = jnp.zeros((8, GROUP * HALF), jnp.float32)
        delta = jnp.zeros((8, GROUP * HALF), jnp.float32)
        for off, size in TILES:
            p = jnp.exp2((s_ref[off:off + size] - top) * (SCALE * LOG2E))
            s_ref[off:off + size] = p
            total = total + fold(p, jnp.add)
            delta = delta + fold(p * g_ref[off:off + size], jnp.add)
        inverse = 1.0 / jnp.sum(total, axis=0, keepdims=True)
        delta = jnp.sum(delta, axis=0, keepdims=True) * inverse
        dq = jnp.zeros((HD, GROUP * HALF), jnp.float32)
        for off, size in TILES:
            p = s_ref[off:off + size] * inverse
            ds = (p * (g_ref[off:off + size] - delta)).astype(jnp.bfloat16)
            to = pl.ds((WINDOW - off - size) // HALF, size // HALF)
            dk = jnp.dot(ds, qb, preferred_element_type=jnp.float32)
            dv = jnp.dot(p.astype(jnp.bfloat16), dob, preferred_element_type=jnp.float32)
            dkw[n, to] = dk.reshape(size // HALF, HALF, HD)
            dvw[n, to] = dv.reshape(size // HALF, HALF, HD)
            dq = dq + dot_tn(tile(kpos, off, size), ds)
        dq = (dq * SCALE).T.astype(jnp.bfloat16)
        for i in range(GROUP):
            dq_v[xs, rows, i * HD:(i + 1) * HD] = dq[i * HALF:(i + 1) * HALF]

    copies = []

    def attend(d):
        if d:
            for j in range(2):
                qd[NX - d, j].wait_recv()
        else:
            loads[3].wait()
            loads[4].wait()

        def side(j, carry):
            row_block(d, j)
            return carry

        lax.fori_loop(0, 2, side, 0)
        if d:
            px = wrap(x + d, NX)
            copy = remote(dq_v.at[px], dq_got.at[x], (dq_send, dq_recv), d - 1, (wide, px * NZ + zl))
            copy.start()
            copies.append(copy)

    attend(0)
    near.advance(3)
    attend(1)

    @pl.when(line.inner)
    def _():
        to_inner.wait_recv()

    @pl.when(line.edge)
    def _():
        to_across.wait_send()
        to_inner.wait_send()

    near.advance(4)
    far.begin()
    attend(3)
    far.begin_second()
    attend(2)
    far.advance(1)

    blocks = [map_ref[j, wrap(x + d, NX) * NZ + zl] for d in range(NX) for j in range(2)]

    def terms_of(z):
        def one(xs, carry):
            slot = z * NX + xs
            for j in range(2):
                p = map_ref[j, xs * NZ + z]
                sums = [jnp.zeros((HALF, HD), jnp.float32)] * 2
                for n, block in enumerate(blocks):
                    step = p - block + BACK
                    inside = (step >= 0) & (step <= BACK)
                    at = jnp.minimum(jnp.maximum(step, 0), BACK)
                    sums = [a + jnp.where(inside, b[n, at], 0.0) for a, b in zip(sums, (dkw, dvw))]
                rows = pl.ds(j * HALF, HALF)
                terms_v[slot, 0, rows] = (sums[0] * SCALE).astype(jnp.bfloat16)
                terms_v[slot, 1, rows] = sums[1].astype(jnp.bfloat16)
            return carry

        lax.fori_loop(0, NX, one, 0)

    def far_term(n, d):
        return terms_v.at[far_z[n] * NX + wrap(x + d, NX)]

    def pass_copy(n, d):
        return remote(far_term(n, d), passed.at[n, d], (pass_send, pass_recv), 2 * d + n, partner)

    def sum_copy(n, d):
        return remote(far_term(n, d), terms_got.at[2, x], (sum_send, sum_recv), 2 * d + n,
                      (wide, wrap(x + d, NX) * NZ + far_z[n]))

    for n in range(2):
        terms_of(far_z[n])

        @pl.when(line.edge)
        def _():
            for d in range(NX):
                pass_copy(n, d).start()

    terms_of(line.partner)
    for d in range(NX):
        px = wrap(x + d, NX)
        copy = remote(terms_v.at[line.partner * NX + px], terms_got.at[1, x], (t_send, t_recv), d,
                      (wide, px * NZ + line.partner))
        copy.start()
        copies.append(copy)
    terms_of(zl)
    for d in (2, 1, 3):
        px = wrap(x + d, NX)
        copy = remote(terms_v.at[zl * NX + px], terms_got.at[0, x], (t_send, t_recv), 3 + d, (wide, px * NZ + zl))
        copy.start()
        copies.append(copy)
    stores = [
        pltpu.make_async_copy(dq_v.at[x], dq_got.at[x], local_sem.at[6]),
        pltpu.make_async_copy(terms_v.at[own_slot], terms_got.at[0, x], local_sem.at[7]),
    ]
    for copy in stores:
        copy.start()

    def combine(n):
        @pl.when(line.inner)
        def _():
            for d in range(NX):
                pass_copy(n, d).wait_recv()
                slot = far_z[n] * NX + wrap(x + d, NX)
                total = terms_v[slot].astype(jnp.float32) + passed[n, d].astype(jnp.float32)
                terms_v[slot] = total.astype(jnp.bfloat16)
                sum_copy(n, d).start()

    combine(0)
    far.advance(2)
    combine(1)
    loads[5].wait()
    near.wait_core(near.core_copies)
    lax.fori_loop(0, NY, project_near, 0)
    far.advance(3)
    far.wait_core(far.core_copies[:10])
    lax.fori_loop(0, 5, project_far, 0)
    far.advance(4)
    far.wait_core(far.core_copies[10:])
    lax.fori_loop(5, NY, project_far, 0)
    projected[...] = acc[...].astype(jnp.bfloat16)
    for copy in copies:
        copy.wait()
    own_kind = (zl // 2 + zl % 2 + 1) % 2
    for d in range(NX):
        remote(passed.at[0, d], passed.at[0, d], (sum_send, sum_recv), 2 * d + own_kind, partner).wait_recv()

    @pl.when(line.edge)
    def _():
        for d in range(NX):
            for n in range(2):
                pass_copy(n, d).wait_send()

    @pl.when(line.inner)
    def _():
        for d in range(NX):
            for n in range(2):
                relay_copy(n, d).wait_send()
                sum_copy(n, d).wait_send()

    for copy in list(kx.values()) + kz + list(qd.values()):
        copy.wait_send()
    near.finish_sends()
    far.finish_sends()
    for copy in stores:
        copy.wait()


def finish_kernel(dq_got, terms_got, projected, dq, dk, dv, kref, vref, dq_v, terms_v, sems):
    x_load = pltpu.make_async_copy(dq_got, dq_v, sems.at[0])
    t_load = pltpu.make_async_copy(terms_got, terms_v, sems.at[1])
    x_load.start()
    t_load.start()
    kref[0] = projected[:, :512]
    vref[0] = projected[:, 512:]
    x_load.wait()
    for xs in range(NX):
        dq[0, :, xs * 512:(xs + 1) * 512] = dq_v[xs].astype(jnp.float32)
    t_load.wait()
    for xs in range(NX):
        for j, out in enumerate((dk, dv)):
            total = terms_v[0, xs, j].astype(jnp.float32)
            for n in (1, 2):
                total = total + terms_v[n, xs, j].astype(jnp.float32)
            out[0, :, xs * HD:(xs + 1) * HD] = total


def body(q_pol, k_pol, v_pol, d_out, h_ref, norm_gain, w_kv_ref, lengths, block_map):
    bf16, f32 = jnp.bfloat16, jnp.float32
    hbm = pl.BlockSpec(memory_space=pltpu.HBM)
    vmem = pl.BlockSpec(memory_space=pltpu.VMEM)
    smem = pl.BlockSpec(memory_space=pltpu.SMEM)
    dma = pltpu.SemaphoreType.DMA
    shape = jax.ShapeDtypeStruct
    heads = (NX, ROWS, GROUP * HD)
    dq_got, terms_got, projected = pl.pallas_call(
        step_kernel,
        name="step",
        out_shape=(shape(heads, bf16), shape((3, NX, 2, ROWS, HD), bf16), shape((ROWS, 1024), bf16)),
        in_specs=[smem, smem] + [hbm] * 6 + [vmem],
        out_specs=(hbm, hbm, vmem),
        scratch_shapes=[
            pltpu.VMEM(heads, bf16),
            pltpu.VMEM(heads, bf16),
            pltpu.VMEM((NX * NZ, 2, ROWS, HD), bf16),
            pltpu.VMEM((BACK + 2 * NX * NZ, HALF, HD), bf16),
            pltpu.VMEM((BACK + 2 * NX * NZ, HALF, HD), bf16),
            pltpu.VMEM((WINDOW, GROUP * HALF), f32),
            pltpu.VMEM((WINDOW, GROUP * HALF), f32),
            pltpu.VMEM((2 * NX, BACK + 1, HALF, HD), f32),
            pltpu.VMEM((2 * NX, BACK + 1, HALF, HD), f32),
            pltpu.VMEM((NX * NZ, 2, ROWS, HD), bf16),
            pltpu.VMEM(heads, bf16),
            pltpu.VMEM((2, NX, 2, ROWS, HD), bf16),
            pltpu.VMEM((NY, 2 * ROWS, 1024), bf16),
            pltpu.VMEM((NY, 2 * ROWS, 1024), bf16),
            pltpu.VMEM((ROWS, 4096), bf16),
            pltpu.VMEM((ROWS, 4096), bf16),
            pltpu.VMEM((ROWS, 1024), f32),
        ]
        + [dma((n,)) for n in (6, 6, 6, 6, 8, 16, 8, 2, 2, 3, 3, 7, 7, 8, 8, 8, 8, 16, 16, 18, 18, 16, 16, 18, 18, 8)],
        compiler_params=pltpu.CompilerParams(collective_id=0, has_side_effects=True, vmem_limit_bytes=VMEM_ALL),
    )(block_map.T, lengths, q_pol, k_pol, v_pol, d_out, w_kv_ref, h_ref, norm_gain.reshape(1, -1))
    return pl.pallas_call(
        finish_kernel,
        name="finish",
        out_shape=(
            shape((1, ROWS, 2048), f32),
            shape((1, ROWS, 512), f32),
            shape((1, ROWS, 512), f32),
            shape((1, ROWS, 512), bf16),
            shape((1, ROWS, 512), bf16),
        ),
        in_specs=[hbm, hbm, vmem],
        out_specs=(vmem,) * 5,
        scratch_shapes=[pltpu.VMEM(heads, bf16), pltpu.VMEM((3, NX, 2, ROWS, HD), bf16), dma((2,))],
        compiler_params=pltpu.CompilerParams(vmem_limit_bytes=VMEM_ALL),
    )(dq_got, terms_got, projected)


def solution(mesh):
    rows = P("wide", "ctx", None)
    return jax.shard_map(
        body,
        mesh=mesh,
        in_specs=(rows, rows, rows, rows, rows, P(), P("wide", None), P("wide", None), P()),
        out_specs=(rows,) * 5,
        check_vma=False,
    )
```

```python
import functools
import jax
import jax.numpy as jnp
from jax import lax
from jax.experimental import pallas as pl
from jax.experimental.pallas import tpu as pltpu
from jax.sharding import PartitionSpec as P

MESH = pl.DeviceIdType.MESH
HD = 128
NX, NZ, NY = 4, 4, 8
GROUP = 4
ROWS = 128
HALF = 64
SCALE = HD ** -0.5
TK = 256
WINDOW = 1024 + HALF
BACK = WINDOW // HALF - 1
TILES = tuple((off, min(TK, WINDOW - off)) for off in range(0, WINDOW, TK))
NEG = -1e30
LOG2E = 1.4426950408889634
MIB = 1 << 20
VMEM_ALL = 63 * MIB


def wrap(value, size):
    return lax.rem(value + size, size)


def place():
    wide = lax.axis_index("wide")
    ctx = lax.axis_index("ctx")
    return wide // 4, (wide // 2) % 2, wide % 2, ctx // NZ, ctx % NZ


def wide_id(y, zh, core):
    return (y * 2 + zh) * 2 + core


def ctx_peers(x, zl):
    peers = []
    for dz in (2, 1, 3, 0):
        for dx in (2, 1, 3, 0):
            if dz or dx:
                peers.append((wrap(x + dx, NX), wrap(zl + dz, NZ)))
    return peers


def meet(ids):
    barrier = pltpu.get_barrier_semaphore()
    for ident in ids:
        pl.semaphore_signal(barrier, inc=1, device_id=ident, device_id_type=MESH)
    pl.semaphore_wait(barrier, len(ids))


def remote(src, dst, sems, slot, ident):
    send, recv = sems
    return pltpu.make_async_remote_copy(
        src_ref=src, dst_ref=dst, send_sem=send.at[slot], recv_sem=recv.at[slot],
        device_id=ident, device_id_type=MESH,
    )


class WeightRing:
    def __init__(self, own, held, ring_sems, core_sems, core_dst=None):
        y, zh, core, x, zl = place()
        ctx = lax.axis_index("ctx")
        self.y, self.core = y, core
        self.own, self.held = own, held
        self.ring_sems, self.core_sems = ring_sems, core_sems
        self.right = (wide_id(wrap(y + 1, NY), zh, core), ctx)
        self.left = (wide_id(wrap(y - 1, NY), zh, core), ctx)
        self.other = (wide_id(y, zh, 1 - core), ctx)
        self.sent = []
        self.core_copies = []

    def chunk(self, owner, core, part):
        start = pl.multiple_of(core * ROWS + part * HALF, HALF)
        return self.held.at[owner, pl.ds(start, HALF)]

    def ring_copy(self, way, step, part):
        owner = wrap(self.y - (step - 1), NY) if way == 0 else wrap(self.y + (step - 1), NY)
        if step == 1:
            src = self.own.at[pl.ds(part * HALF, HALF)]
        else:
            src = self.chunk(owner, self.core, part)
        slot = (step - 1) * 4 + way * 2 + part
        return remote(src, self.chunk(owner, self.core, part), self.ring_sems, slot,
                      self.right if way == 0 else self.left)

    def arrival(self, way, step, part):
        owner = wrap(self.y - step, NY) if way == 0 else wrap(self.y + step, NY)
        dst = self.chunk(owner, self.core, part)
        slot = (step - 1) * 4 + way * 2 + part
        return remote(dst, dst, self.ring_sems, slot, self.right if way == 0 else self.left)

    def core_slot(self, way, step, part):
        return (step - 1) * 4 + way * 2 + part + 2

    def to_core(self, src, owner, part, slot):
        copy = remote(src, self.chunk(owner, self.core, part), self.core_sems, slot, self.other)
        copy.start()
        self.core_copies.append((copy, owner, part, slot))

    def valid(self, way, step, part):
        return step < 4 or (step == 4 and part == way)

    def begin(self):
        for way in range(2):
            copy = self.ring_copy(way, 1, 0)
            copy.start()
            self.sent.append(copy)
        for part in range(2):
            self.to_core(self.own.at[pl.ds(part * HALF, HALF)], self.y, part, part)

    def begin_second(self):
        for copy in self.sent[:2]:
            copy.wait_send()
        for way in range(2):
            copy = self.ring_copy(way, 1, 1)
            copy.start()
            self.sent.append(copy)

    def advance(self, step):
        for part in range(2):
            for way in range(2):
                if self.valid(way, step, part):
                    self.arrival(way, step, part).wait_recv()
                    if self.valid(way, step + 1, part):
                        copy = self.ring_copy(way, step + 1, part)
                        copy.start()
                        self.sent.append(copy)
                    owner = wrap(self.y - step, NY) if way == 0 else wrap(self.y + step, NY)
                    self.to_core(self.chunk(owner, self.core, part), owner, part, self.core_slot(way, step, part))

    def wait_core(self, copies):
        for copy, owner, part, slot in copies:
            dst = self.chunk(owner, 1 - self.core, part)
            remote(dst, dst, self.core_sems, slot, self.other).wait_recv()

    def finish_sends(self):
        for copy in self.sent[2:]:
            copy.wait_send()
        for copy, _, _, _ in self.core_copies:
            copy.wait_send()


class Line:
    def __init__(self, zl):
        half = zl // 2
        self.partner = zl + 1 - 2 * (zl % 2)
        self.far_inner = 2 - half
        self.far_edge = 3 - 3 * half
        self.edge = (zl == 0) | (zl == NZ - 1)
        self.inner = (zl == 1) | (zl == 2)


def cols(index, width):
    return pl.ds(pl.multiple_of(index * width, width), width)


def dot_nt(a, b):
    return lax.dot_general(a, b, (((1,), (1,)), ((), ())), preferred_element_type=jnp.float32)


def dot_tn(a, b):
    return lax.dot_general(a, b, (((0,), (0,)), ((), ())), preferred_element_type=jnp.float32)


def fold(values, combine):
    parts = [values[i:i + 8] for i in range(0, values.shape[0], 8)]
    while len(parts) > 1:
        parts = [combine(parts[i], parts[i + 1]) if i + 1 < len(parts) else parts[i] for i in range(0, len(parts), 2)]
    return parts[0]


def step_kernel(map_ref, len_ref, q, k, v, do, w, h, gain, dq_got, terms_got, projected,
                q_v, do_v, kv_v, kpos, vpos, s_ref, g_ref, dkw, dvw, terms_v, dq_v, passed,
                near_v, far_v, h_v, normed, acc,
                x_send, x_recv, kx_send, kx_recv, kz_send, kz_recv, relay_send, zh_send, zh_recv,
                dq_send, dq_recv, t_send, t_recv, pass_send, pass_recv, sum_send, sum_recv,
                near_send, near_recv, near_csend, near_crecv, far_send, far_recv, far_csend, far_crecv, local_sem):
    y, zh, core, x, zl = place()
    wide = lax.axis_index("wide")
    line = Line(zl)
    own_rows = pl.ds(pl.multiple_of(core * ROWS, ROWS), ROWS)
    own_slot = zl * NX + x
    loads = [
        pltpu.make_async_copy(k.at[0, :, cols(x, HD)], kv_v.at[own_slot, 0], local_sem.at[0]),
        pltpu.make_async_copy(v.at[0, :, cols(x, HD)], kv_v.at[own_slot, 1], local_sem.at[1]),
        pltpu.make_async_copy(h.at[0], h_v, local_sem.at[2]),
        pltpu.make_async_copy(q.at[0, :, cols(x, GROUP * HD)], q_v.at[x], local_sem.at[3]),
        pltpu.make_async_copy(do.at[0, :, cols(x, GROUP * HD)], do_v.at[x], local_sem.at[4]),
        pltpu.make_async_copy(w, near_v.at[y, own_rows], local_sem.at[5]),
    ]
    for copy in loads:
        copy.start()
    near = WeightRing(w, near_v, (near_send, near_recv), (near_csend, near_crecv))
    far_own = far_v.at[y, own_rows]
    far = WeightRing(far_own, far_v, (far_send, far_recv), (far_csend, far_crecv))
    across = (wide_id(y, 1 - zh, core), x * NZ + (NZ - 1 - zl))
    partner = (wide, x * NZ + line.partner)
    far_inner = (wide, x * NZ + line.far_inner)
    far_z = (line.far_inner, line.far_edge)
    meet([(wide, px * NZ + pz) for px, pz in ctx_peers(x, zl)] + [near.right, near.left, near.other, across])

    kx = {}
    for d in (1, 3, 2):
        px = wrap(x + d, NX)
        for j, src in enumerate((k, v)):
            kx[d, j] = remote(src.at[0, :, cols(px, HD)], kv_v.at[own_slot, j], (kx_send, kx_recv), 2 * (d - 1) + j,
                              (wide, px * NZ + zl))
            kx[d, j].start()
    to_across = remote(w, far_own, (zh_send, zh_recv), 0, across)
    to_inner = remote(far_own, far_own, (zh_send, zh_recv), 1, partner)
    pl.when(line.edge)(to_across.start)
    near.begin()

    def piece(z, d, send_sem, ident):
        slot = z * NX + wrap(x + d, NX)
        return pltpu.make_async_remote_copy(
            src_ref=kv_v.at[slot], dst_ref=kv_v.at[slot], send_sem=send_sem, recv_sem=kz_recv.at[slot],
            device_id=ident, device_id_type=MESH,
        )

    kz = []

    def along(d):
        for n, ident in enumerate((far_inner, partner)):
            copy = piece(zl, d, kz_send.at[2 * d + n], ident)
            copy.start()
            kz.append(copy)

    def arrived(z, d):
        piece(z, d, kz_send.at[0], partner).wait_recv()

    def relay_copy(n, d):
        return piece(far_z[n], d, relay_send.at[2 * d + n], partner)

    def relay(d):
        @pl.when(line.inner)
        def _():
            for n in range(2):
                arrived(far_z[n], d)
                relay_copy(n, d).start()

    loads[0].wait()
    loads[1].wait()
    along(0)
    for d in (1, 3, 2):
        for j in range(2):
            kx[d, j].wait_recv()
        along(NX - d)
    qd = {}
    for d in (1, 3, 2):
        px = wrap(x + d, NX)
        for j, (src, dst) in enumerate(((q, q_v), (do, do_v))):
            qd[d, j] = remote(src.at[0, :, cols(px, GROUP * HD)], dst.at[x], (x_send, x_recv), 2 * (d - 1) + j,
                              (wide, px * NZ + zl))
            qd[d, j].start()
    relay(0)
    near.begin_second()

    kpos[pl.ds(0, BACK)] = jnp.zeros((BACK, HALF, HD), jnp.bfloat16)
    vpos[pl.ds(0, BACK)] = jnp.zeros((BACK, HALF, HD), jnp.bfloat16)
    relay(3)
    near.advance(1)

    @pl.when(line.edge)
    def _():
        to_across.wait_recv()
        to_inner.start()

    relay(1)
    loads[2].wait()
    strip = 16
    scale_by = gain[...].astype(jnp.float32)

    def norm_rows(i, carry):
        rows = pl.ds(pl.multiple_of(i * strip, strip), strip)
        a = h_v[rows].astype(jnp.float32)
        mean = jnp.mean(a * a, axis=1, keepdims=True)
        a = a * lax.rsqrt(mean + 1e-05)
        for c in range(a.shape[1] // HD):
            at = slice(c * HD, (c + 1) * HD)
            normed[rows, at] = (a[:, at] * scale_by[c:c + 1]).astype(jnp.bfloat16)
        return carry

    lax.fori_loop(0, ROWS // strip, norm_rows, 0)
    acc[...] = jnp.zeros_like(acc)
    near.advance(2)
    relay(2)

    @pl.when(line.inner)
    def _():
        to_inner.wait_recv()

    far.begin()

    def project(weights, zh_of, owner):
        at = pl.ds(pl.multiple_of((2 * owner + zh_of) * 2 * ROWS, 2 * ROWS), 2 * ROWS)
        acc[...] += jnp.dot(normed[:, at], weights[owner], preferred_element_type=jnp.float32)

    def project_near(i, carry):
        project(near_v, zh, wrap(y + i - 2 + NY, NY))
        return carry

    def project_far(i, carry):
        project(far_v, 1 - zh, wrap(y + i - 2 + NY, NY))
        return carry

    @pl.when(line.edge)
    def _():
        for d in (0, 3, 1, 2):
            for n in range(2):
                arrived(far_z[n], d)

    for d in range(NX):
        arrived(line.partner, d)

    def place_block(p, carry):
        slot = jnp.int32(0)
        for i in range(NX * NZ):
            slot = jnp.where(map_ref[0, i] == p, (i % NZ) * NX + i // NZ, slot)
        for j, dst in enumerate((kpos, vpos)):
            pair = kv_v[slot, j]
            dst[BACK + p] = pair[:HALF]
            dst[BACK + 2 * NX * NZ - 1 - p] = pair[HALF:]
        return carry

    lax.fori_loop(0, NX * NZ, place_block, 0)
    ends = [len_ref[0, 0]]
    for i in range(1, 4):
        ends.append(ends[-1] + len_ref[0, i])

    def doc_start(pos):
        start = jnp.zeros_like(pos)
        for end in ends:
            start = jnp.where(pos >= end, end, start)
        return start

    def row_block(d, j):
        xs = wrap(x + d, NX)
        n = 2 * d + j
        block = map_ref[j, xs * NZ + zl]
        base = block * HALF
        rows = pl.ds(pl.multiple_of(j * HALF, HALF), HALF)
        qb = jnp.concatenate([q_v[xs, rows, i * HD:(i + 1) * HD] for i in range(GROUP)], axis=0)
        dob = jnp.concatenate([do_v[xs, rows, i * HD:(i + 1) * HD] for i in range(GROUP)], axis=0)
        lane = lax.broadcasted_iota(jnp.int32, (1, GROUP * HALF), 1)
        pos = base + lane % HALF
        first = doc_start(pos)
        top = jnp.full((8, GROUP * HALF), NEG, jnp.float32)

        def tile(ref, off, size):
            first_block = block + (WINDOW - off - size) // HALF
            parts = [ref[first_block + i] for i in range(size // HALF)]
            return jnp.concatenate(parts, axis=0) if len(parts) > 1 else parts[0]

        for off, size in TILES:
            kp = base + HALF - off - size + lax.broadcasted_iota(jnp.int32, (size, GROUP * HALF), 0)
            s = jnp.where((kp <= pos) & (kp >= first), dot_nt(tile(kpos, off, size), qb), NEG)
            s_ref[off:off + size] = s
            g_ref[off:off + size] = dot_nt(tile(vpos, off, size), dob)
            top = jnp.maximum(top, fold(s, jnp.maximum))
        top = jnp.max(top, axis=0, keepdims=True)
        total = jnp.zeros((8, GROUP * HALF), jnp.float32)
        delta = jnp.zeros((8, GROUP * HALF), jnp.float32)
        for off, size in TILES:
            p = jnp.exp2((s_ref[off:off + size] - top) * (SCALE * LOG2E))
            s_ref[off:off + size] = p
            total = total + fold(p, jnp.add)
            delta = delta + fold(p * g_ref[off:off + size], jnp.add)
        inverse = 1.0 / jnp.sum(total, axis=0, keepdims=True)
        delta = jnp.sum(delta, axis=0, keepdims=True) * inverse
        dq = jnp.zeros((HD, GROUP * HALF), jnp.float32)
        for off, size in TILES:
            p = s_ref[off:off + size] * inverse
            ds = (p * (g_ref[off:off + size] - delta)).astype(jnp.bfloat16)
            to = pl.ds((WINDOW - off - size) // HALF, size // HALF)
            dk = jnp.dot(ds, qb, preferred_element_type=jnp.float32)
            dv = jnp.dot(p.astype(jnp.bfloat16), dob, preferred_element_type=jnp.float32)
            dkw[n, to] = dk.reshape(size // HALF, HALF, HD)
            dvw[n, to] = dv.reshape(size // HALF, HALF, HD)
            dq = dq + dot_tn(tile(kpos, off, size), ds)
        dq = (dq * SCALE).T.astype(jnp.bfloat16)
        for i in range(GROUP):
            dq_v[xs, rows, i * HD:(i + 1) * HD] = dq[i * HALF:(i + 1) * HALF]

    copies = []

    def attend(d):
        if d:
            for j in range(2):
                qd[NX - d, j].wait_recv()
        else:
            loads[3].wait()
            loads[4].wait()

        def side(j, carry):
            row_block(d, j)
            return carry

        lax.fori_loop(0, 2, side, 0)
        if d:
            px = wrap(x + d, NX)
            copy = remote(dq_v.at[px], dq_got.at[x], (dq_send, dq_recv), d - 1, (wide, px * NZ + zl))
            copy.start()
            copies.append(copy)

    attend(0)
    near.advance(3)
    far.begin_second()
    attend(1)
    far.advance(1)
    attend(3)
    near.advance(4)
    attend(2)
    far.advance(2)

    @pl.when(line.edge)
    def _():
        to_across.wait_send()
        to_inner.wait_send()

    blocks = [map_ref[j, wrap(x + d, NX) * NZ + zl] for d in range(NX) for j in range(2)]

    def terms_of(z):
        def one(xs, carry):
            slot = z * NX + xs
            for j in range(2):
                p = map_ref[j, xs * NZ + z]
                sums = [jnp.zeros((HALF, HD), jnp.float32)] * 2
                for n, block in enumerate(blocks):
                    step = p - block + BACK
                    inside = (step >= 0) & (step <= BACK)
                    at = jnp.minimum(jnp.maximum(step, 0), BACK)
                    sums = [a + jnp.where(inside, b[n, at], 0.0) for a, b in zip(sums, (dkw, dvw))]
                rows = pl.ds(j * HALF, HALF)
                terms_v[slot, 0, rows] = (sums[0] * SCALE).astype(jnp.bfloat16)
                terms_v[slot, 1, rows] = sums[1].astype(jnp.bfloat16)
            return carry

        lax.fori_loop(0, NX, one, 0)

    def far_term(n, d):
        return terms_v.at[far_z[n] * NX + wrap(x + d, NX)]

    def pass_copy(n, d):
        return remote(far_term(n, d), passed.at[n, d], (pass_send, pass_recv), 2 * d + n, partner)

    def sum_copy(n, d):
        return remote(far_term(n, d), terms_got.at[2, x], (sum_send, sum_recv), 2 * d + n,
                      (wide, wrap(x + d, NX) * NZ + far_z[n]))

    for n in range(2):
        terms_of(far_z[n])

        @pl.when(line.edge)
        def _():
            for d in range(NX):
                pass_copy(n, d).start()

    terms_of(line.partner)
    for d in range(NX):
        px = wrap(x + d, NX)
        copy = remote(terms_v.at[line.partner * NX + px], terms_got.at[1, x], (t_send, t_recv), d,
                      (wide, px * NZ + line.partner))
        copy.start()
        copies.append(copy)
    terms_of(zl)
    for d in (2, 1, 3):
        px = wrap(x + d, NX)
        copy = remote(terms_v.at[zl * NX + px], terms_got.at[0, x], (t_send, t_recv), 3 + d, (wide, px * NZ + zl))
        copy.start()
        copies.append(copy)
    stores = [
        pltpu.make_async_copy(dq_v.at[x], dq_got.at[x], local_sem.at[6]),
        pltpu.make_async_copy(terms_v.at[own_slot], terms_got.at[0, x], local_sem.at[7]),
    ]
    for copy in stores:
        copy.start()

    def combine(n):
        @pl.when(line.inner)
        def _():
            for d in range(NX):
                pass_copy(n, d).wait_recv()
                slot = far_z[n] * NX + wrap(x + d, NX)
                total = terms_v[slot].astype(jnp.float32) + passed[n, d].astype(jnp.float32)
                terms_v[slot] = total.astype(jnp.bfloat16)
                sum_copy(n, d).start()

    loads[5].wait()
    near.wait_core(near.core_copies)
    lax.fori_loop(0, NY, project_near, 0)
    combine(0)
    far.advance(3)
    combine(1)
    far.wait_core(far.core_copies[:10])
    lax.fori_loop(0, 5, project_far, 0)
    far.advance(4)
    far.wait_core(far.core_copies[10:])
    lax.fori_loop(5, NY, project_far, 0)
    projected[...] = acc[...].astype(jnp.bfloat16)
    for copy in copies:
        copy.wait()
    own_kind = (zl // 2 + zl % 2 + 1) % 2
    for d in range(NX):
        remote(passed.at[0, d], passed.at[0, d], (sum_send, sum_recv), 2 * d + own_kind, partner).wait_recv()

    @pl.when(line.edge)
    def _():
        for d in range(NX):
            for n in range(2):
                pass_copy(n, d).wait_send()

    @pl.when(line.inner)
    def _():
        for d in range(NX):
            for n in range(2):
                relay_copy(n, d).wait_send()
                sum_copy(n, d).wait_send()

    for copy in list(kx.values()) + kz + list(qd.values()):
        copy.wait_send()
    near.finish_sends()
    far.finish_sends()
    for copy in stores:
        copy.wait()


def finish_kernel(dq_got, terms_got, projected, dq, dk, dv, kref, vref,
                  dq_v, terms_v, p_v, dq_f, dkv_f, kv_f, load_sems, store_sems):
    x_loads = [pltpu.make_async_copy(dq_got.at[xs], dq_v.at[xs], load_sems.at[xs]) for xs in range(NX)]
    t_load = pltpu.make_async_copy(terms_got, terms_v, load_sems.at[NX])
    p_load = pltpu.make_async_copy(projected, p_v, load_sems.at[NX + 1])
    stores = []

    def store(src, dst):
        copy = pltpu.make_async_copy(src, dst, store_sems.at[len(stores)])
        copy.start()
        stores.append(copy)

    for copy in x_loads:
        copy.start()
    t_load.start()
    p_load.start()
    for xs in range(NX):
        x_loads[xs].wait()
        at = pl.ds(xs * GROUP * HD, GROUP * HD)
        dq_f[xs] = dq_v[xs].astype(jnp.float32)
        store(dq_f.at[xs], dq.at[0, :, at])
    t_load.wait()
    for j, out in enumerate((dk, dv)):
        for xs in range(NX):
            total = terms_v[0, xs, j].astype(jnp.float32)
            for n in (1, 2):
                total = total + terms_v[n, xs, j].astype(jnp.float32)
            dkv_f[j, :, xs * HD:(xs + 1) * HD] = total
        store(dkv_f.at[j], out.at[0])
    p_load.wait()
    for j, out in enumerate((kref, vref)):
        kv_f[j] = p_v[:, j * 512:(j + 1) * 512]
        store(kv_f.at[j], out.at[0])
    for copy in stores:
        copy.wait()


def body(q_pol, k_pol, v_pol, d_out, h_ref, norm_gain, w_kv_ref, lengths, block_map):
    bf16, f32 = jnp.bfloat16, jnp.float32
    hbm = pl.BlockSpec(memory_space=pltpu.HBM)
    vmem = pl.BlockSpec(memory_space=pltpu.VMEM)
    smem = pl.BlockSpec(memory_space=pltpu.SMEM)
    dma = pltpu.SemaphoreType.DMA
    shape = jax.ShapeDtypeStruct
    heads = (NX, ROWS, GROUP * HD)
    dq_got, terms_got, projected = pl.pallas_call(
        step_kernel,
        name="step",
        out_shape=(shape(heads, bf16), shape((3, NX, 2, ROWS, HD), bf16), shape((ROWS, 1024), bf16)),
        in_specs=[smem, smem] + [hbm] * 6 + [vmem],
        out_specs=(hbm, hbm, vmem),
        scratch_shapes=[
            pltpu.VMEM(heads, bf16),
            pltpu.VMEM(heads, bf16),
            pltpu.VMEM((NX * NZ, 2, ROWS, HD), bf16),
            pltpu.VMEM((BACK + 2 * NX * NZ, HALF, HD), bf16),
            pltpu.VMEM((BACK + 2 * NX * NZ, HALF, HD), bf16),
            pltpu.VMEM((WINDOW, GROUP * HALF), f32),
            pltpu.VMEM((WINDOW, GROUP * HALF), f32),
            pltpu.VMEM((2 * NX, BACK + 1, HALF, HD), f32),
            pltpu.VMEM((2 * NX, BACK + 1, HALF, HD), f32),
            pltpu.VMEM((NX * NZ, 2, ROWS, HD), bf16),
            pltpu.VMEM(heads, bf16),
            pltpu.VMEM((2, NX, 2, ROWS, HD), bf16),
            pltpu.VMEM((NY, 2 * ROWS, 1024), bf16),
            pltpu.VMEM((NY, 2 * ROWS, 1024), bf16),
            pltpu.VMEM((ROWS, 4096), bf16),
            pltpu.VMEM((ROWS, 4096), bf16),
            pltpu.VMEM((ROWS, 1024), f32),
        ]
        + [dma((n,)) for n in (6, 6, 6, 6, 8, 16, 8, 2, 2, 3, 3, 7, 7, 8, 8, 8, 8, 16, 16, 18, 18, 16, 16, 18, 18, 8)],
        compiler_params=pltpu.CompilerParams(collective_id=0, has_side_effects=True, vmem_limit_bytes=VMEM_ALL),
    )(block_map.T, lengths, q_pol, k_pol, v_pol, d_out, w_kv_ref, h_ref, norm_gain.reshape(-1, HD))
    return pl.pallas_call(
        finish_kernel,
        name="finish",
        out_shape=(
            shape((1, ROWS, 2048), f32),
            shape((1, ROWS, 512), f32),
            shape((1, ROWS, 512), f32),
            shape((1, ROWS, 512), bf16),
            shape((1, ROWS, 512), bf16),
        ),
        in_specs=[hbm] * 3,
        out_specs=(hbm,) * 5,
        scratch_shapes=[
            pltpu.VMEM(heads, bf16),
            pltpu.VMEM((3, NX, 2, ROWS, HD), bf16),
            pltpu.VMEM((ROWS, 1024), bf16),
            pltpu.VMEM(heads, f32),
            pltpu.VMEM((2, ROWS, 512), f32),
            pltpu.VMEM((2, ROWS, 512), bf16),
            dma((NX + 2,)),
            dma((NX + 4,)),
        ],
        compiler_params=pltpu.CompilerParams(vmem_limit_bytes=VMEM_ALL),
    )(dq_got, terms_got, projected)


def solution(mesh):
    rows = P("wide", "ctx", None)
    return jax.shard_map(
        body,
        mesh=mesh,
        in_specs=(rows, rows, rows, rows, rows, P(), P("wide", None), P("wide", None), P()),
        out_specs=(rows,) * 5,
        check_vma=False,
    )
```

```python
import functools
import jax
import jax.numpy as jnp
from jax import lax
from jax.experimental import pallas as pl
from jax.experimental.pallas import tpu as pltpu
from jax.sharding import PartitionSpec as P

MESH = pl.DeviceIdType.MESH
HD = 128
NX, NZ, NY = 4, 4, 8
GROUP = 4
ROWS = 128
HALF = 64
SCALE = HD ** -0.5
TK = 256
WINDOW = 1024 + HALF
BACK = WINDOW // HALF - 1
TILES = tuple((off, min(TK, WINDOW - off)) for off in range(0, WINDOW, TK))
NEG = -1e30
LOG2E = 1.4426950408889634
MIB = 1 << 20
VMEM_ALL = 63 * MIB


def wrap(value, size):
    return lax.rem(value + size, size)


def place():
    wide = lax.axis_index("wide")
    ctx = lax.axis_index("ctx")
    return wide // 4, (wide // 2) % 2, wide % 2, ctx // NZ, ctx % NZ


def wide_id(y, zh, core):
    return (y * 2 + zh) * 2 + core


def ctx_peers(x, zl):
    peers = []
    for dz in (2, 1, 3, 0):
        for dx in (2, 1, 3, 0):
            if dz or dx:
                peers.append((wrap(x + dx, NX), wrap(zl + dz, NZ)))
    return peers


def meet(ids):
    barrier = pltpu.get_barrier_semaphore()
    for ident in ids:
        pl.semaphore_signal(barrier, inc=1, device_id=ident, device_id_type=MESH)
    pl.semaphore_wait(barrier, len(ids))


def remote(src, dst, sems, slot, ident):
    send, recv = sems
    return pltpu.make_async_remote_copy(
        src_ref=src, dst_ref=dst, send_sem=send.at[slot], recv_sem=recv.at[slot],
        device_id=ident, device_id_type=MESH,
    )


class WeightRing:
    def __init__(self, own, held, ring_sems, core_sems, core_dst=None):
        y, zh, core, x, zl = place()
        ctx = lax.axis_index("ctx")
        self.y, self.core = y, core
        self.own, self.held = own, held
        self.ring_sems, self.core_sems = ring_sems, core_sems
        self.right = (wide_id(wrap(y + 1, NY), zh, core), ctx)
        self.left = (wide_id(wrap(y - 1, NY), zh, core), ctx)
        self.other = (wide_id(y, zh, 1 - core), ctx)
        self.sent = []
        self.core_copies = []

    def chunk(self, owner, core, part):
        start = pl.multiple_of(core * ROWS + part * HALF, HALF)
        return self.held.at[owner, pl.ds(start, HALF)]

    def ring_copy(self, way, step, part):
        owner = wrap(self.y - (step - 1), NY) if way == 0 else wrap(self.y + (step - 1), NY)
        if step == 1:
            src = self.own.at[pl.ds(part * HALF, HALF)]
        else:
            src = self.chunk(owner, self.core, part)
        slot = (step - 1) * 4 + way * 2 + part
        return remote(src, self.chunk(owner, self.core, part), self.ring_sems, slot,
                      self.right if way == 0 else self.left)

    def arrival(self, way, step, part):
        owner = wrap(self.y - step, NY) if way == 0 else wrap(self.y + step, NY)
        dst = self.chunk(owner, self.core, part)
        slot = (step - 1) * 4 + way * 2 + part
        return remote(dst, dst, self.ring_sems, slot, self.right if way == 0 else self.left)

    def core_slot(self, way, step, part):
        return (step - 1) * 4 + way * 2 + part + 2

    def to_core(self, src, owner, part, slot):
        copy = remote(src, self.chunk(owner, self.core, part), self.core_sems, slot, self.other)
        copy.start()
        self.core_copies.append((copy, owner, part, slot))

    def valid(self, way, step, part):
        return step < 4 or (step == 4 and part == way)

    def begin(self):
        for part in range(2):
            for way in range(2):
                copy = self.ring_copy(way, 1, part)
                copy.start()
                self.sent.append(copy)
        for part in range(2):
            self.to_core(self.own.at[pl.ds(part * HALF, HALF)], self.y, part, part)

    def advance(self, step):
        for part in range(2):
            for way in range(2):
                if self.valid(way, step, part):
                    self.arrival(way, step, part).wait_recv()
                    if self.valid(way, step + 1, part):
                        copy = self.ring_copy(way, step + 1, part)
                        copy.start()
                        self.sent.append(copy)
                    owner = wrap(self.y - step, NY) if way == 0 else wrap(self.y + step, NY)
                    self.to_core(self.chunk(owner, self.core, part), owner, part, self.core_slot(way, step, part))

    def wait_core(self, copies):
        for copy, owner, part, slot in copies:
            dst = self.chunk(owner, 1 - self.core, part)
            remote(dst, dst, self.core_sems, slot, self.other).wait_recv()

    def finish_sends(self):
        for copy in self.sent:
            copy.wait_send()
        for copy, _, _, _ in self.core_copies:
            copy.wait_send()


class Line:
    def __init__(self, zl):
        half = zl // 2
        self.partner = zl + 1 - 2 * (zl % 2)
        self.far_inner = 2 - half
        self.far_edge = 3 - 3 * half
        self.edge = (zl == 0) | (zl == NZ - 1)
        self.inner = (zl == 1) | (zl == 2)


def cols(index, width):
    return pl.ds(pl.multiple_of(index * width, width), width)


def dot_nt(a, b):
    return lax.dot_general(a, b, (((1,), (1,)), ((), ())), preferred_element_type=jnp.float32)


def dot_tn(a, b):
    return lax.dot_general(a, b, (((0,), (0,)), ((), ())), preferred_element_type=jnp.float32)


def fold(values, combine):
    parts = [values[i:i + 8] for i in range(0, values.shape[0], 8)]
    while len(parts) > 1:
        parts = [combine(parts[i], parts[i + 1]) if i + 1 < len(parts) else parts[i] for i in range(0, len(parts), 2)]
    return parts[0]


def step_kernel(map_ref, len_ref, q, k, v, do, w, h, gain, dq_got, terms_got, projected,
                q_v, do_v, kv_v, kpos, vpos, s_ref, g_ref, s2_ref, g2_ref, dkw, dvw, terms_v, dq_v, passed,
                near_v, far_v, h_v, normed, acc,
                x_send, x_recv, kx_send, kx_recv, kz_send, kz_recv, relay_send, zh_send, zh_recv,
                dq_send, dq_recv, t_send, t_recv, pass_send, pass_recv, sum_send, sum_recv,
                near_send, near_recv, near_csend, near_crecv, far_send, far_recv, far_csend, far_crecv, local_sem):
    y, zh, core, x, zl = place()
    wide = lax.axis_index("wide")
    line = Line(zl)
    own_rows = pl.ds(pl.multiple_of(core * ROWS, ROWS), ROWS)
    own_slot = zl * NX + x
    loads = [
        pltpu.make_async_copy(k.at[0, :, cols(x, HD)], kv_v.at[own_slot, 0], local_sem.at[0]),
        pltpu.make_async_copy(v.at[0, :, cols(x, HD)], kv_v.at[own_slot, 1], local_sem.at[1]),
        pltpu.make_async_copy(h.at[0], h_v, local_sem.at[2]),
        pltpu.make_async_copy(q.at[0, :, cols(x, GROUP * HD)], q_v.at[x], local_sem.at[3]),
        pltpu.make_async_copy(do.at[0, :, cols(x, GROUP * HD)], do_v.at[x], local_sem.at[4]),
        pltpu.make_async_copy(w, near_v.at[y, own_rows], local_sem.at[5]),
    ]
    for copy in loads:
        copy.start()
    near = WeightRing(w, near_v, (near_send, near_recv), (near_csend, near_crecv))
    far_own = far_v.at[y, own_rows]
    far = WeightRing(far_own, far_v, (far_send, far_recv), (far_csend, far_crecv))
    across = (wide_id(y, 1 - zh, core), x * NZ + (NZ - 1 - zl))
    partner = (wide, x * NZ + line.partner)
    far_inner = (wide, x * NZ + line.far_inner)
    far_z = (line.far_inner, line.far_edge)
    meet([(wide, px * NZ + pz) for px, pz in ctx_peers(x, zl)] + [near.right, near.left, near.other, across])

    kx = {}
    for d in (1, 3, 2):
        px = wrap(x + d, NX)
        for j, src in enumerate((k, v)):
            kx[d, j] = remote(src.at[0, :, cols(px, HD)], kv_v.at[own_slot, j], (kx_send, kx_recv), 2 * (d - 1) + j,
                              (wide, px * NZ + zl))
            kx[d, j].start()
    to_across = remote(w, far_own, (zh_send, zh_recv), 0, across)
    to_inner = remote(far_own, far_own, (zh_send, zh_recv), 1, partner)
    pl.when(line.edge)(to_across.start)
    near.begin()

    def piece(z, d, send_sem, ident):
        slot = z * NX + wrap(x + d, NX)
        return pltpu.make_async_remote_copy(
            src_ref=kv_v.at[slot], dst_ref=kv_v.at[slot], send_sem=send_sem, recv_sem=kz_recv.at[slot],
            device_id=ident, device_id_type=MESH,
        )

    kz = []

    def along(d):
        for n, ident in enumerate((far_inner, partner)):
            copy = piece(zl, d, kz_send.at[2 * d + n], ident)
            copy.start()
            kz.append(copy)

    def arrived(z, d):
        piece(z, d, kz_send.at[0], partner).wait_recv()

    def relay_copy(n, d):
        return piece(far_z[n], d, relay_send.at[2 * d + n], partner)

    def relay(d):
        @pl.when(line.inner)
        def _():
            for n in range(2):
                arrived(far_z[n], d)
                relay_copy(n, d).start()

    loads[0].wait()
    loads[1].wait()
    along(0)
    for d in (1, 3, 2):
        for j in range(2):
            kx[d, j].wait_recv()
        along(NX - d)
    qd = {}
    for d in (1, 3, 2):
        px = wrap(x + d, NX)
        for j, (src, dst) in enumerate(((q, q_v), (do, do_v))):
            qd[d, j] = remote(src.at[0, :, cols(px, GROUP * HD)], dst.at[x], (x_send, x_recv), 2 * (d - 1) + j,
                              (wide, px * NZ + zl))
            qd[d, j].start()
    relay(0)

    kpos[pl.ds(0, BACK)] = jnp.zeros((BACK, HALF, HD), jnp.bfloat16)
    vpos[pl.ds(0, BACK)] = jnp.zeros((BACK, HALF, HD), jnp.bfloat16)
    near.advance(1)
    relay(3)

    @pl.when(line.edge)
    def _():
        to_across.wait_recv()
        to_inner.start()

    relay(1)
    loads[2].wait()
    strip = 16
    scale_by = gain[...].astype(jnp.float32)

    def norm_rows(i, carry):
        rows = pl.ds(pl.multiple_of(i * strip, strip), strip)
        a = h_v[rows].astype(jnp.float32)
        mean = jnp.mean(a * a, axis=1, keepdims=True)
        a = a * lax.rsqrt(mean + 1e-05)
        for c in range(a.shape[1] // HD):
            at = slice(c * HD, (c + 1) * HD)
            normed[rows, at] = (a[:, at] * scale_by[c:c + 1]).astype(jnp.bfloat16)
        return carry

    lax.fori_loop(0, ROWS // strip, norm_rows, 0)
    acc[...] = jnp.zeros_like(acc)
    near.advance(2)
    relay(2)

    @pl.when(line.inner)
    def _():
        to_inner.wait_recv()

    far.begin()

    def project(weights, zh_of, owner):
        at = pl.ds(pl.multiple_of((2 * owner + zh_of) * 2 * ROWS, 2 * ROWS), 2 * ROWS)
        acc[...] += jnp.dot(normed[:, at], weights[owner], preferred_element_type=jnp.float32)

    def project_near(i, carry):
        project(near_v, zh, wrap(y + i - 2 + NY, NY))
        return carry

    def project_far(i, carry):
        project(far_v, 1 - zh, wrap(y + i - 2 + NY, NY))
        return carry

    @pl.when(line.edge)
    def _():
        for d in (0, 3, 1, 2):
            for n in range(2):
                arrived(far_z[n], d)

    for d in range(NX):
        arrived(line.partner, d)

    def place_block(p, carry):
        slot = jnp.int32(0)
        for i in range(NX * NZ):
            slot = jnp.where(map_ref[0, i] == p, (i % NZ) * NX + i // NZ, slot)
        for j, dst in enumerate((kpos, vpos)):
            pair = kv_v[slot, j]
            dst[BACK + p] = pair[:HALF]
            dst[BACK + 2 * NX * NZ - 1 - p] = pair[HALF:]
        return carry

    lax.fori_loop(0, NX * NZ, place_block, 0)
    near.advance(3)
    ends = [len_ref[0, 0]]
    for i in range(1, 4):
        ends.append(ends[-1] + len_ref[0, i])

    def doc_start(pos):
        start = jnp.zeros_like(pos)
        for end in ends:
            start = jnp.where(pos >= end, end, start)
        return start

    class Block:
        def __init__(self, d, j, buffers):
            self.xs, self.n = wrap(x + d, NX), 2 * d + j
            self.rows = slice(j * HALF, (j + 1) * HALF)
            self.s, self.g = buffers
            self.block = map_ref[j, self.xs * NZ + zl]
            self.base = self.block * HALF
            self.q = self.heads(q_v)
            self.do = self.heads(do_v)
            lane = lax.broadcasted_iota(jnp.int32, (1, GROUP * HALF), 1)
            self.pos = self.base + lane % HALF
            self.first = doc_start(self.pos)
            self.top = jnp.full((8, GROUP * HALF), NEG, jnp.float32)
            self.total = jnp.zeros((8, GROUP * HALF), jnp.float32)
            self.delta = jnp.zeros((8, GROUP * HALF), jnp.float32)
            self.dq = jnp.zeros((HD, GROUP * HALF), jnp.float32)

        def heads(self, ref):
            return jnp.concatenate([ref[self.xs, self.rows, i * HD:(i + 1) * HD] for i in range(GROUP)], axis=0)

        def tile(self, ref, off, size):
            start = self.block + (WINDOW - off - size) // HALF
            parts = [ref[start + i] for i in range(size // HALF)]
            return jnp.concatenate(parts, axis=0) if len(parts) > 1 else parts[0]

        def score(self, off, size):
            kp = self.base + HALF - off - size + lax.broadcasted_iota(jnp.int32, (size, GROUP * HALF), 0)
            seen = kp >= self.first
            if off == 0:
                seen = seen & (kp <= self.pos)
            s = jnp.where(seen, dot_nt(self.tile(kpos, off, size), self.q), NEG)
            self.s[off:off + size] = s
            self.g[off:off + size] = dot_nt(self.tile(vpos, off, size), self.do)
            self.top = jnp.maximum(self.top, fold(s, jnp.maximum))

        def start_weigh(self):
            self.top = jnp.max(self.top, axis=0, keepdims=True)

        def weigh(self, off, size):
            p = jnp.exp2((self.s[off:off + size] - self.top) * (SCALE * LOG2E))
            self.s[off:off + size] = p
            self.total = self.total + fold(p, jnp.add)
            self.delta = self.delta + fold(p * self.g[off:off + size], jnp.add)

        def start_grads(self):
            self.inverse = 1.0 / jnp.sum(self.total, axis=0, keepdims=True)
            self.delta = jnp.sum(self.delta, axis=0, keepdims=True) * self.inverse

        def grads(self, off, size):
            p = self.s[off:off + size] * self.inverse
            ds = (p * (self.g[off:off + size] - self.delta)).astype(jnp.bfloat16)
            to = pl.ds((WINDOW - off - size) // HALF, size // HALF)
            dk = jnp.dot(ds, self.q, preferred_element_type=jnp.float32)
            dv = jnp.dot(p.astype(jnp.bfloat16), self.do, preferred_element_type=jnp.float32)
            dkw[self.n, to] = dk.reshape(size // HALF, HALF, HD)
            dvw[self.n, to] = dv.reshape(size // HALF, HALF, HD)
            self.dq = self.dq + dot_tn(self.tile(kpos, off, size), ds)

        def store(self):
            dq = (self.dq * SCALE).T.astype(jnp.bfloat16)
            for i in range(GROUP):
                dq_v[self.xs, self.rows, i * HD:(i + 1) * HD] = dq[i * HALF:(i + 1) * HALF]

    copies = []

    def lower_block(d):
        if d:
            for j in range(2):
                qd[NX - d, j].wait_recv()
        else:
            loads[3].wait()
            loads[4].wait()
        return Block(d, 0, (s_ref, g_ref))

    def serve(m):
        if m == 1:
            far.advance(1)
        elif m == 2:
            near.advance(4)

    order = (0, 1, 3, 2)
    lower = lower_block(0)
    for t in TILES:
        lower.score(*t)
    for m, d in enumerate(order):
        upper = Block(d, 1, (s2_ref, g2_ref))
        lower.start_weigh()
        for t in TILES:
            lower.weigh(*t)
            upper.score(*t)
        lower.start_grads()
        upper.start_weigh()
        for t in TILES:
            lower.grads(*t)
            upper.weigh(*t)
        lower.store()
        upper.start_grads()
        after = lower_block(order[m + 1]) if m + 1 < NX else None
        for t in TILES:
            upper.grads(*t)
            if after is not None:
                after.score(*t)
        upper.store()
        lower = after
        if d:
            px = wrap(x + d, NX)
            copy = remote(dq_v.at[px], dq_got.at[x], (dq_send, dq_recv), d - 1, (wide, px * NZ + zl))
            copy.start()
            copies.append(copy)
        serve(m)

    @pl.when(line.edge)
    def _():
        to_across.wait_send()
        to_inner.wait_send()

    blocks = [map_ref[j, wrap(x + d, NX) * NZ + zl] for d in range(NX) for j in range(2)]

    def terms_of(z):
        def one(xs, carry):
            slot = z * NX + xs
            for j in range(2):
                p = map_ref[j, xs * NZ + z]
                sums = [jnp.zeros((HALF, HD), jnp.float32)] * 2
                for n, block in enumerate(blocks):
                    step = p - block + BACK
                    inside = (step >= 0) & (step <= BACK)
                    at = jnp.minimum(jnp.maximum(step, 0), BACK)
                    sums = [a + jnp.where(inside, b[n, at], 0.0) for a, b in zip(sums, (dkw, dvw))]
                rows = pl.ds(j * HALF, HALF)
                terms_v[slot, 0, rows] = (sums[0] * SCALE).astype(jnp.bfloat16)
                terms_v[slot, 1, rows] = sums[1].astype(jnp.bfloat16)
            return carry

        lax.fori_loop(0, NX, one, 0)

    def far_term(n, d):
        return terms_v.at[far_z[n] * NX + wrap(x + d, NX)]

    def pass_copy(n, d):
        return remote(far_term(n, d), passed.at[n, d], (pass_send, pass_recv), 2 * d + n, partner)

    def sum_copy(n, d):
        return remote(far_term(n, d), terms_got.at[2, x], (sum_send, sum_recv), 2 * d + n,
                      (wide, wrap(x + d, NX) * NZ + far_z[n]))

    for n in range(2):
        terms_of(far_z[n])

        @pl.when(line.edge)
        def _():
            for d in range(NX):
                pass_copy(n, d).start()

    terms_of(line.partner)
    for d in range(NX):
        px = wrap(x + d, NX)
        copy = remote(terms_v.at[line.partner * NX + px], terms_got.at[1, x], (t_send, t_recv), d,
                      (wide, px * NZ + line.partner))
        copy.start()
        copies.append(copy)
    terms_of(zl)
    for d in (2, 1, 3):
        px = wrap(x + d, NX)
        copy = remote(terms_v.at[zl * NX + px], terms_got.at[0, x], (t_send, t_recv), 3 + d, (wide, px * NZ + zl))
        copy.start()
        copies.append(copy)
    stores = [
        pltpu.make_async_copy(dq_v.at[x], dq_got.at[x], local_sem.at[6]),
        pltpu.make_async_copy(terms_v.at[own_slot], terms_got.at[0, x], local_sem.at[7]),
    ]
    for copy in stores:
        copy.start()

    def combine(n):
        @pl.when(line.inner)
        def _():
            for d in range(NX):
                pass_copy(n, d).wait_recv()
                slot = far_z[n] * NX + wrap(x + d, NX)
                total = terms_v[slot].astype(jnp.float32) + passed[n, d].astype(jnp.float32)
                terms_v[slot] = total.astype(jnp.bfloat16)
                sum_copy(n, d).start()

    far.advance(2)
    loads[5].wait()
    near.wait_core(near.core_copies)
    lax.fori_loop(0, NY, project_near, 0)
    combine(0)
    far.advance(3)
    combine(1)
    far.wait_core(far.core_copies[:10])
    lax.fori_loop(0, 5, project_far, 0)
    far.advance(4)
    far.wait_core(far.core_copies[10:])
    lax.fori_loop(5, NY, project_far, 0)
    projected[...] = acc[...].astype(jnp.bfloat16)
    for copy in copies:
        copy.wait()
    own_kind = (zl // 2 + zl % 2 + 1) % 2
    for d in range(NX):
        remote(passed.at[0, d], passed.at[0, d], (sum_send, sum_recv), 2 * d + own_kind, partner).wait_recv()

    @pl.when(line.edge)
    def _():
        for d in range(NX):
            for n in range(2):
                pass_copy(n, d).wait_send()

    @pl.when(line.inner)
    def _():
        for d in range(NX):
            for n in range(2):
                relay_copy(n, d).wait_send()
                sum_copy(n, d).wait_send()

    for copy in list(kx.values()) + kz + list(qd.values()):
        copy.wait_send()
    near.finish_sends()
    far.finish_sends()
    for copy in stores:
        copy.wait()


def finish_kernel(dq_got, terms_got, projected, dq, dk, dv, kref, vref,
                  dq_v, terms_v, p_v, dq_f, dkv_f, kv_f, load_sems, store_sems):
    x_loads = [pltpu.make_async_copy(dq_got.at[xs], dq_v.at[xs], load_sems.at[xs]) for xs in range(NX)]
    t_load = pltpu.make_async_copy(terms_got, terms_v, load_sems.at[NX])
    p_load = pltpu.make_async_copy(projected, p_v, load_sems.at[NX + 1])
    stores = []

    def store(src, dst):
        copy = pltpu.make_async_copy(src, dst, store_sems.at[len(stores)])
        copy.start()
        stores.append(copy)

    for copy in x_loads:
        copy.start()
    t_load.start()
    p_load.start()
    for xs in range(NX):
        x_loads[xs].wait()
        at = pl.ds(xs * GROUP * HD, GROUP * HD)
        dq_f[xs] = dq_v[xs].astype(jnp.float32)
        store(dq_f.at[xs], dq.at[0, :, at])
    t_load.wait()
    for j, out in enumerate((dk, dv)):
        for xs in range(NX):
            total = terms_v[0, xs, j].astype(jnp.float32)
            for n in (1, 2):
                total = total + terms_v[n, xs, j].astype(jnp.float32)
            dkv_f[j, :, xs * HD:(xs + 1) * HD] = total
        store(dkv_f.at[j], out.at[0])
    p_load.wait()
    for j, out in enumerate((kref, vref)):
        kv_f[j] = p_v[:, j * 512:(j + 1) * 512]
        store(kv_f.at[j], out.at[0])
    for copy in stores:
        copy.wait()


def body(q_pol, k_pol, v_pol, d_out, h_ref, norm_gain, w_kv_ref, lengths, block_map):
    bf16, f32 = jnp.bfloat16, jnp.float32
    hbm = pl.BlockSpec(memory_space=pltpu.HBM)
    vmem = pl.BlockSpec(memory_space=pltpu.VMEM)
    smem = pl.BlockSpec(memory_space=pltpu.SMEM)
    dma = pltpu.SemaphoreType.DMA
    shape = jax.ShapeDtypeStruct
    heads = (NX, ROWS, GROUP * HD)
    dq_got, terms_got, projected = pl.pallas_call(
        step_kernel,
        name="step",
        out_shape=(shape(heads, bf16), shape((3, NX, 2, ROWS, HD), bf16), shape((ROWS, 1024), bf16)),
        in_specs=[smem, smem] + [hbm] * 6 + [vmem],
        out_specs=(hbm, hbm, vmem),
        scratch_shapes=[
            pltpu.VMEM(heads, bf16),
            pltpu.VMEM(heads, bf16),
            pltpu.VMEM((NX * NZ, 2, ROWS, HD), bf16),
            pltpu.VMEM((BACK + 2 * NX * NZ, HALF, HD), bf16),
            pltpu.VMEM((BACK + 2 * NX * NZ, HALF, HD), bf16),
            pltpu.VMEM((WINDOW, GROUP * HALF), f32),
            pltpu.VMEM((WINDOW, GROUP * HALF), f32),
            pltpu.VMEM((WINDOW, GROUP * HALF), f32),
            pltpu.VMEM((WINDOW, GROUP * HALF), f32),
            pltpu.VMEM((2 * NX, BACK + 1, HALF, HD), f32),
            pltpu.VMEM((2 * NX, BACK + 1, HALF, HD), f32),
            pltpu.VMEM((NX * NZ, 2, ROWS, HD), bf16),
            pltpu.VMEM(heads, bf16),
            pltpu.VMEM((2, NX, 2, ROWS, HD), bf16),
            pltpu.VMEM((NY, 2 * ROWS, 1024), bf16),
            pltpu.VMEM((NY, 2 * ROWS, 1024), bf16),
            pltpu.VMEM((ROWS, 4096), bf16),
            pltpu.VMEM((ROWS, 4096), bf16),
            pltpu.VMEM((ROWS, 1024), f32),
        ]
        + [dma((n,)) for n in (6, 6, 6, 6, 8, 16, 8, 2, 2, 3, 3, 7, 7, 8, 8, 8, 8, 16, 16, 18, 18, 16, 16, 18, 18, 8)],
        compiler_params=pltpu.CompilerParams(collective_id=0, has_side_effects=True, vmem_limit_bytes=VMEM_ALL),
    )(block_map.T, lengths, q_pol, k_pol, v_pol, d_out, w_kv_ref, h_ref, norm_gain.reshape(-1, HD))
    return pl.pallas_call(
        finish_kernel,
        name="finish",
        out_shape=(
            shape((1, ROWS, 2048), f32),
            shape((1, ROWS, 512), f32),
            shape((1, ROWS, 512), f32),
            shape((1, ROWS, 512), bf16),
            shape((1, ROWS, 512), bf16),
        ),
        in_specs=[hbm] * 3,
        out_specs=(hbm,) * 5,
        scratch_shapes=[
            pltpu.VMEM(heads, bf16),
            pltpu.VMEM((3, NX, 2, ROWS, HD), bf16),
            pltpu.VMEM((ROWS, 1024), bf16),
            pltpu.VMEM(heads, f32),
            pltpu.VMEM((2, ROWS, 512), f32),
            pltpu.VMEM((2, ROWS, 512), bf16),
            dma((NX + 2,)),
            dma((NX + 4,)),
        ],
        compiler_params=pltpu.CompilerParams(vmem_limit_bytes=VMEM_ALL),
    )(dq_got, terms_got, projected)


def solution(mesh):
    rows = P("wide", "ctx", None)
    return jax.shard_map(
        body,
        mesh=mesh,
        in_specs=(rows, rows, rows, rows, rows, P(), P("wide", None), P("wide", None), P()),
        out_specs=(rows,) * 5,
        check_vma=False,
    )
```
